256 devices in a mesh: rows: 32 (over y, z), rrep: 8 (over x, core).
Axes of the slice: x: 4, y: 4, z: 8, core: 2. Of those that a mesh axis runs over, the one named last changes fastest.
Arguments:
- features: bfloat16 [49152, 1024], P(('rows', 'rrep')), may hold values from -6 to 6
- labels: int32 [49152], P(('rows', 'rrep')), may hold values from 0 to 999
- scores: bfloat16 [49152, 1000], P(('rows', 'rrep')), may hold values from -4 to 4
- landmarks: bfloat16 [16384, 1024], P('rows'), may hold values from -6 to 6
- coefficients: float32 [16384, 1000], P('rows'), may hold values from -4 to 4
- block_ids: int32 [2], replicated, may hold values from 0 to 31
Outputs:
- new_coefficients: float32 [16384, 1000], P('rows')
- residual: float32 [49152, 1000], P(('rows', 'rrep'))
The draws below stay inside these ranges and needn't reach their ends.
Inputs may be any that keep to these rules, and one draw needn't show every extreme that they name: `block_ids`: index of a landmark block; blocks may repeat.
All inputs are finite; a program needn't handle non-finite values.
Results may differ from the reference program's by a relative error of at most 0.003.
Values may be sent and summed in bfloat16 or wider, within the bound.
A program may use at most 128 MiB of HBM per device.

```python
import jax
import jax.numpy as jnp
from jax import lax

F = 1024
C = 1000
BLOCK = 512
STEPS = 2
NROWS = 49152
LANDMARKS = 16384
N_ROWS = 32


def set_ends(entries, stream_key, low, largest):
    longest = entries.shape.index(max(entries.shape))
    spots = []
    for shift in (0, 1):
        where = [jax.random.randint(jax.random.fold_in(stream_key, axis), (), 0, length) for axis, length in enumerate(entries.shape)]
        where[longest] = (where[longest] + shift) % entries.shape[longest]
        spots.append(tuple(where))
    return entries.at[spots[0]].set(low).at[spots[1]].set(largest)


def steps_of(rng, dims, cuts, smallest, high):
    def one(axis_at, blocks):
        draws = jax.random.uniform(jax.random.fold_in(jax.random.fold_in(rng, 6), axis_at), (blocks,), jnp.float32, smallest / len(cuts), high / len(cuts))
        return jnp.repeat(jnp.exp(draws), dims[axis_at] // blocks).reshape((-1,) + (1,) * (len(dims) - axis_at - 1))

    level = one(*cuts[0])
    for cut in cuts[1:]:
        level = level * one(*cut)
    return level


def scatter_about(key, extent, deviation, bound, cuts=(), kind=jnp.bfloat16):
    entries = jax.random.normal(key, extent, jnp.float32) * deviation
    if len(cuts) > 0:
        entries = steps_of(key, extent, cuts, -0.22, 0.18) * entries
    return jnp.clip(entries, min=-bound, max=bound).astype(kind)


def setup_inputs(seed: int = 0) -> dict:
    streams_of = jax.random.split(jax.random.key(seed), 7)
    return {
        "features": scatter_about(streams_of[0], (NROWS, F), 1.0, 6.0, ((0, 256),)),
        "labels": set_ends(jax.random.randint(streams_of[1], (NROWS,), 0, C), jax.random.fold_in(streams_of[1], 1), 0, C - 1).astype(jnp.int32),
        "scores": scatter_about(streams_of[2], (NROWS, C), 0.5, 4.0, ((0, 256),)),
        "landmarks": scatter_about(streams_of[3], (LANDMARKS, F), 1.0, 6.0, ((0, 32),)),
        "coefficients": scatter_about(streams_of[4], (LANDMARKS, C), 0.5, 4.0, ((0, 32),), jnp.float32),
        "block_ids": jax.random.randint(streams_of[5], (STEPS,), 0, N_ROWS).astype(jnp.int32),
    }


def unit_normalize(values):
    wide = values.astype(jnp.float32)
    scale = lax.rsqrt(lax.optimization_barrier(jnp.mean(wide * wide, axis=1, keepdims=True)) + 1e-06)
    return (wide * scale).astype(jnp.bfloat16)

def reference(features, labels, scores, landmarks, coefficients, block_ids):
    feature_estimate = unit_normalize(features)
    zhat = unit_normalize(landmarks)
    classes = jnp.arange(C, dtype=jnp.int32)
    residual = (labels[:, None] == classes[None, :]).astype(jnp.float32) - scores.astype(jnp.float32)
    new_coefficients = coefficients
    ridge = jnp.float32(NROWS) * jnp.eye(BLOCK, dtype=jnp.float32)
    for step in range(STEPS):
        start = (block_ids[step] * BLOCK).astype(jnp.int32)
        landmark_slab = lax.dynamic_slice_in_dim(zhat, start, BLOCK, 0)
        inner_product = lax.dot_general(feature_estimate.astype(jnp.float32), landmark_slab.astype(jnp.float32), (((1,), (1,)), ((), ())), preferred_element_type=jnp.float32)
        kern = jnp.exp(inner_product * F ** (-0.5)).astype(jnp.bfloat16)
        gram = lax.dot_general(kern.astype(jnp.float32), kern.astype(jnp.float32), (((0,), (0,)), ((), ())), preferred_element_type=jnp.float32)
        rounded = residual.astype(jnp.bfloat16)
        product = lax.dot_general(kern.astype(jnp.float32), rounded.astype(jnp.float32), (((0,), (0,)), ((), ())), preferred_element_type=jnp.float32)
        cholesky_factor = jnp.linalg.cholesky(gram + ridge)
        delta = jax.scipy.linalg.cho_solve((cholesky_factor, True), product)
        current = lax.dynamic_slice_in_dim(new_coefficients, start, BLOCK, 0)
        new_coefficients = lax.dynamic_update_slice_in_dim(new_coefficients, current + delta, start, 0)
        residual = residual - jnp.dot(kern.astype(jnp.float32), delta.astype(jnp.bfloat16).astype(jnp.float32), preferred_element_type=jnp.float32)
    return (new_coefficients, residual)
```

```python
import functools

import jax
import jax.numpy as jnp
from jax import lax
from jax.experimental import pallas as pl
from jax.experimental.pallas import tpu as pltpu
from jax.sharding import PartitionSpec as P

MESH = pl.DeviceIdType.MESH
HI = lax.Precision.HIGHEST
F32 = jnp.float32
BF16 = jnp.bfloat16
NX, NY, NZ = 4, 4, 8
BLOCK = 512
CLASSES = 1024
VMEM_LIMIT = 48 * 2**20


class Place:
    def __init__(self):
        rows, rrep = lax.axis_index("rows"), lax.axis_index("rrep")
        self.rows, self.rrep = rows, rrep
        self.y, self.z = rows // NZ, rows % NZ
        self.x, self.c = rrep // 2, rrep % 2

    def at_x(self, d):
        other = (self.x + d) % NX
        return other, (self.rows, other * 2 + self.c)

    def at_y(self, d):
        other = (self.y + d) % NY
        return other, (other * NZ + self.z, self.rrep)

    def at_z(self, d):
        other = (self.z + d) % NZ
        return other, (self.y * NZ + other, self.rrep)

    def partner(self):
        return (self.rows, self.x * 2 + 1 - self.c)

    def greet(self, axes):
        barrier = pltpu.get_barrier_semaphore()
        peers = []
        if "x" in axes:
            peers += [self.at_x(d)[1] for d in range(1, NX)]
        if "y" in axes:
            peers += [self.at_y(d)[1] for d in range(1, NY)]
        if "z" in axes:
            peers += [self.at_z(d)[1] for d in range(1, NZ)]
        if "c" in axes:
            peers += [self.partner()]
        for peer in peers:
            pl.semaphore_signal(barrier, inc=1, device_id=peer, device_id_type=MESH)
        pl.semaphore_wait(barrier, len(peers))


class Sender:
    def __init__(self, send_sems, recv_sems):
        self.send_sems, self.recv_sems = send_sems, recv_sems
        self.copies = []

    def start(self, src, dst, device):
        i = len(self.copies)
        copy = pltpu.make_async_remote_copy(
            src_ref=src,
            dst_ref=dst,
            send_sem=self.send_sems.at[i],
            recv_sem=self.recv_sems.at[i],
            device_id=device,
            device_id_type=MESH,
        )
        copy.start()
        self.copies.append(copy)
        return copy

    def drain(self):
        for copy in self.copies:
            copy.wait_send()


def arrive(copies):
    for copy in copies:
        copy.wait_recv()


LAND_COPIES = 2 + 3 + 7 + 7 + 6 + 6 + 1


def land_kernel(zin, xin, rin, zout, xp, rp, r1, s1, r2, send_sems, recv_sems):
    me = Place()
    me.greet("xyzc")
    out = Sender(send_sems, recv_sems)
    x, y, z, c = me.x, me.y, me.z, me.c
    first = []
    for d in range(1, NY):
        other, device = me.at_y(d)
        first.append(out.start(zin.at[other], r1.at[d - 1], device))
    swap = [out.start(xin, xp, me.partner()), out.start(rin, rp, me.partner())]
    arrive(first)
    s1[...] = zin[y] + r1[0] + r1[1] + r1[2]
    second = []
    for d in range(1, NZ):
        other, device = me.at_z(d)
        second.append(out.start(s1.at[other], r2.at[d - 1], device))
    arrive(second)
    total = s1[z]
    for d in range(1, NZ):
        total = total + r2[d - 1]
    s, g = z // 4, z % 4
    zout[y, s, x, c, g] = total
    third = []
    for d in range(1, NZ):
        _, device = me.at_z(d)
        third.append(out.start(zout.at[y, s, x, c, g], zout.at[y, s, x, c, g], device))
    arrive(third)
    fourth = []
    for d in range(1, 4):
        fourth.append(out.start(zout.at[y, 0, x, c], zout.at[y, 0, x, c], me.at_y(d)[1]))
        fourth.append(out.start(zout.at[y, 1, x, c], zout.at[y, 1, x, c], me.at_x(d)[1]))
    arrive(fourth)
    fifth = []
    for d in range(1, 4):
        fifth.append(out.start(zout.at[:, 0, x, c], zout.at[:, 0, x, c], me.at_x(d)[1]))
        fifth.append(out.start(zout.at[y, 1, :, c], zout.at[y, 1, :, c], me.at_y(d)[1]))
    arrive(fifth)
    last = out.start(zout.at[:, :, :, c], zout.at[:, :, :, c], me.partner())
    arrive([last])
    arrive(swap)
    out.drain()


def land(zin, xhat, rounded):
    rows = xhat.shape[0]
    vmem = pl.BlockSpec(memory_space=pltpu.VMEM)
    return pl.pallas_call(
        land_kernel,
        out_shape=(
            jax.ShapeDtypeStruct((NY, 2, NX, 2, 4, 16, 256), BF16),
            jax.ShapeDtypeStruct((rows, 1024), BF16),
            jax.ShapeDtypeStruct((rows, CLASSES), BF16),
        ),
        in_specs=[vmem] * 3,
        out_specs=(vmem,) * 3,
        scratch_shapes=[
            pltpu.VMEM((NY - 1, NZ, 16, 256), BF16),
            pltpu.VMEM((NZ, 16, 256), BF16),
            pltpu.VMEM((NZ - 1, 16, 256), BF16),
            pltpu.SemaphoreType.DMA((LAND_COPIES,)),
            pltpu.SemaphoreType.DMA((LAND_COPIES,)),
        ],
        compiler_params=pltpu.CompilerParams(
            collective_id=0, has_side_effects=True, vmem_limit_bytes=VMEM_LIMIT
        ),
        name="land",
    )(zin, xhat, rounded)


def partial_kernel(zall, xo, xp, ro, rp, kout, gout, pout, kern, resid):
    rows = xo.shape[0]
    c = lax.axis_index("rrep") % 2
    for half, xref in enumerate((xo, xp)):
        total = None
        for y in range(NY):
            zy = zall[y].reshape(2 * BLOCK, 256)
            part = lax.dot_general(
                xref[:, y * 256 : (y + 1) * 256],
                zy,
                (((1,), (1,)), ((), ())),
                preferred_element_type=F32,
            )
            total = part if total is None else total + part
        kern[half * rows : (half + 1) * rows, :] = jnp.exp(total * (1024**-0.5)).astype(BF16)
    kout[...] = kern[:rows, :]
    resid[:rows, :] = ro[...]
    resid[rows:, :] = rp[...]
    contract = (((0,), (0,)), ((), ()))
    mine = kern[:, pl.ds(pl.multiple_of(c * BLOCK, BLOCK), BLOCK)]
    cross = kern[:, pl.ds(pl.multiple_of(BLOCK + c * 256, 256), 256)]
    for y in range(NY):
        cols = kern[:, pl.ds(pl.multiple_of(c * BLOCK + y * 128, 128), 128)]
        first = kern[:, y * 128 : (y + 1) * 128]
        gram = lax.dot_general(mine, cols, contract, preferred_element_type=F32)
        side = lax.dot_general(cross, first, contract, preferred_element_type=F32)
        both = jnp.concatenate([gram, side], axis=0)
        for x in range(NX):
            gout[x, y] = both[x * 192 : (x + 1) * 192].reshape(NZ, 24, 128)
    for k in range(4):
        prod = lax.dot_general(
            resid[:, k * 256 : (k + 1) * 256], mine, contract, preferred_element_type=F32
        )
        pout[k] = prod.astype(BF16).reshape(NY, 64, BLOCK)


def partials(zall, xo, xp, ro, rp):
    rows = xo.shape[0]
    vmem = pl.BlockSpec(memory_space=pltpu.VMEM)
    return pl.pallas_call(
        partial_kernel,
        out_shape=(
            jax.ShapeDtypeStruct((rows, 2 * BLOCK), BF16),
            jax.ShapeDtypeStruct((NX, NY, NZ, 24, 128), F32),
            jax.ShapeDtypeStruct((NX, NY, 64, BLOCK), BF16),
        ),
        in_specs=[vmem] * 5,
        out_specs=(vmem,) * 3,
        scratch_shapes=[
            pltpu.VMEM((2 * rows, 2 * BLOCK), BF16),
            pltpu.VMEM((2 * rows, CLASSES), BF16),
        ],
        compiler_params=pltpu.CompilerParams(vmem_limit_bytes=VMEM_LIMIT),
        name="partials",
    )(zall, xo, xp, ro, rp)


SUM_COPIES = 12 + 12 + 14 + 7 + 6 + 6


def sum_kernel(
    gin, pin, gout, pout, ra, rb, qa, qb, ga, gb, pa, pb, ra2, rb2, qa2, qb2, g2, p2, r3, q3, send_sems, recv_sems
):
    me = Place()
    me.greet("xyz")
    out = Sender(send_sems, recv_sems)
    x, y, z = me.x, me.y, me.z
    copies = []
    for d in range(1, 4):
        i, device = me.at_x(d)
        copies.append(out.start(gin.at[i, :, 0:4], ra.at[d - 1], device))
        copies.append(out.start(pin.at[i, :, 0:32], qa.at[d - 1], device))
        i, device = me.at_y(d)
        copies.append(out.start(gin.at[:, i, 4:8], rb.at[d - 1], device))
        copies.append(out.start(pin.at[:, i, 32:64], qb.at[d - 1], device))
    arrive(copies)
    ga[...] = gin[x, :, 0:4] + ra[0] + ra[1] + ra[2]
    gb[...] = gin[:, y, 4:8] + rb[0] + rb[1] + rb[2]
    wide = lambda value: value.astype(F32)
    pa[...] = (wide(pin[x, :, 0:32]) + wide(qa[0]) + wide(qa[1]) + wide(qa[2])).astype(BF16)
    pb[...] = (wide(pin[:, y, 32:64]) + wide(qb[0]) + wide(qb[1]) + wide(qb[2])).astype(BF16)
    copies = []
    for d in range(1, 4):
        i, device = me.at_y(d)
        copies.append(out.start(ga.at[i], ra2.at[d - 1], device))
        copies.append(out.start(pa.at[i], qa2.at[d - 1], device))
        i, device = me.at_x(d)
        copies.append(out.start(gb.at[i], rb2.at[d - 1], device))
        copies.append(out.start(pb.at[i], qb2.at[d - 1], device))
    arrive(copies)
    g2[0:4] = ga[y] + ra2[0] + ra2[1] + ra2[2]
    g2[4:8] = gb[x] + rb2[0] + rb2[1] + rb2[2]
    sa = wide(pa[y]) + wide(qa2[0]) + wide(qa2[1]) + wide(qa2[2])
    sb = wide(pb[x]) + wide(qb2[0]) + wide(qb2[1]) + wide(qb2[2])
    p2[0:4] = sa.reshape(4, 8, BLOCK)
    p2[4:8] = sb.reshape(4, 8, BLOCK)
    copies = []
    for d in range(1, NZ):
        i, device = me.at_z(d)
        copies.append(out.start(g2.at[i], r3.at[d - 1], device))
        copies.append(out.start(p2.at[i], q3.at[d - 1], device))
    arrive(copies)
    gram, prod = g2[z], p2[z]
    for d in range(1, NZ):
        gram = gram + r3[d - 1]
        prod = prod + q3[d - 1]
    gout[x, y, z] = gram
    pout[...] = prod
    copies = []
    for d in range(1, NZ):
        copies.append(out.start(gout.at[x, y, z], gout.at[x, y, z], me.at_z(d)[1]))
    arrive(copies)
    copies = []
    for d in range(1, 4):
        copies.append(out.start(gout.at[x, y, 0:4], gout.at[x, y, 0:4], me.at_y(d)[1]))
        copies.append(out.start(gout.at[x, y, 4:8], gout.at[x, y, 4:8], me.at_x(d)[1]))
    arrive(copies)
    copies = []
    for d in range(1, 4):
        copies.append(out.start(gout.at[x, :, 0:4], gout.at[x, :, 0:4], me.at_x(d)[1]))
        copies.append(out.start(gout.at[:, y, 4:8], gout.at[:, y, 4:8], me.at_y(d)[1]))
    arrive(copies)
    out.drain()


def sums(gram, prod):
    vmem = pl.BlockSpec(memory_space=pltpu.VMEM)
    return pl.pallas_call(
        sum_kernel,
        out_shape=(
            jax.ShapeDtypeStruct((NX, NY, NZ, 24, 128), F32),
            jax.ShapeDtypeStruct((8, BLOCK), F32),
        ),
        in_specs=[vmem] * 2,
        out_specs=(vmem,) * 2,
        scratch_shapes=[
            pltpu.VMEM((3, 4, 4, 24, 128), F32),
            pltpu.VMEM((3, 4, 4, 24, 128), F32),
            pltpu.VMEM((3, 4, 32, BLOCK), BF16),
            pltpu.VMEM((3, 4, 32, BLOCK), BF16),
            pltpu.VMEM((4, 4, 24, 128), F32),
            pltpu.VMEM((4, 4, 24, 128), F32),
            pltpu.VMEM((4, 32, BLOCK), BF16),
            pltpu.VMEM((4, 32, BLOCK), BF16),
            pltpu.VMEM((3, 4, 24, 128), F32),
            pltpu.VMEM((3, 4, 24, 128), F32),
            pltpu.VMEM((3, 32, BLOCK), BF16),
            pltpu.VMEM((3, 32, BLOCK), BF16),
            pltpu.VMEM((NZ, 24, 128), F32),
            pltpu.VMEM((NZ, 8, BLOCK), F32),
            pltpu.VMEM((NZ - 1, 24, 128), F32),
            pltpu.VMEM((NZ - 1, 8, BLOCK), F32),
            pltpu.SemaphoreType.DMA((SUM_COPIES,)),
            pltpu.SemaphoreType.DMA((SUM_COPIES,)),
        ],
        compiler_params=pltpu.CompilerParams(
            collective_id=1, has_side_effects=True, vmem_limit_bytes=VMEM_LIMIT
        ),
        name="sums",
    )(gram, prod)


def eliminate_rows(values, k, n):
    lane = lax.broadcasted_iota(jnp.int32, (8, n), 1)
    sub = lax.broadcasted_iota(jnp.int32, (8, n), 0)
    rows = values[k : k + 8, :]
    pivots = [jnp.broadcast_to(rows[:, k + q : k + q + 1], (8, n)) for q in range(8)]
    inside = (lane >= k) & (lane < k + 8)
    panel = jnp.where(inside, (lane - k == sub).astype(F32), rows)
    for q in range(8):
        factor = pivots[q]
        inverse = 1.0 / jnp.broadcast_to(factor[q : q + 1, :], (8, n))
        own = sub == q

        def update(block):
            row = jnp.broadcast_to(block[q : q + 1, :], (8, n)) * inverse
            return jnp.where(own, row, block - factor * row)

        for j in range(q + 1, 8):
            pivots[j] = update(pivots[j])
        panel = update(panel)
    return panel


def invert_tile(values, n):
    lane = lax.broadcasted_iota(jnp.int32, (n, n), 1)
    for k in range(0, n, 8):
        panel = eliminate_rows(values, k, n)
        inside = (lane >= k) & (lane < k + 8)
        rest = jnp.where(inside, 0.0, values)
        for q in range(8):
            column = jnp.broadcast_to(values[:, k + q : k + q + 1], (n, n))
            rest = rest - column * jnp.broadcast_to(panel[q : q + 1, :], (n, n))
        parts = ([rest[:k]] if k else []) + [panel] + ([rest[k + 8 :]] if k + 8 < n else [])
        values = jnp.concatenate(parts, axis=0)
    return values


def invert(ref, n, tiles):
    b = n // tiles
    for j in range(tiles):
        s = slice(j * b, (j + 1) * b)
        inverse = invert_tile(ref[s, s], b)
        row = jnp.dot(inverse, ref[s, :], precision=HI, preferred_element_type=F32)
        column = ref[:, s]
        ref[:, s] = jnp.zeros((n, b), F32)
        parts = ([row[:, : j * b]] if j else []) + [inverse]
        parts += [row[:, (j + 1) * b :]] if j < tiles - 1 else []
        row = jnp.concatenate(parts, axis=1)
        for i in range(tiles):
            t = slice(i * b, (i + 1) * b)
            if i != j:
                ref[t, :] -= jnp.dot(column[t], row, precision=HI, preferred_element_type=F32)
        ref[s, :] = row


def solve_kernel(ridge, gram, prod, inv, side, delta, part, full):
    for x in range(NX):
        for y in range(NY):
            full[x * 192 : (x + 1) * 192, y * 128 : (y + 1) * 128] = gram[x, y].reshape(192, 128)
    rows = lax.broadcasted_iota(jnp.int32, (BLOCK, BLOCK), 0)
    cols = lax.broadcasted_iota(jnp.int32, (BLOCK, BLOCK), 1)
    inv[...] = full[:BLOCK] + jnp.where(rows == cols, ridge, 0.0)
    side[...] = full[BLOCK:]
    invert(inv, BLOCK, 4)
    first = jnp.dot(prod[...], inv[...], precision=HI, preferred_element_type=F32)
    delta[...] = first
    part[...] = across(first, side[...])


def across(delta, side):
    return lax.dot_general(
        delta.astype(BF16).astype(F32),
        side,
        (((1,), (1,)), ((), ())),
        precision=HI,
        preferred_element_type=F32,
    )


def solve(gram, prod, ridge):
    vmem = pl.BlockSpec(memory_space=pltpu.VMEM)
    return pl.pallas_call(
        functools.partial(solve_kernel, ridge),
        out_shape=(
            jax.ShapeDtypeStruct((BLOCK, BLOCK), F32),
            jax.ShapeDtypeStruct((256, BLOCK), F32),
            jax.ShapeDtypeStruct((8, BLOCK), F32),
            jax.ShapeDtypeStruct((8, 256), F32),
        ),
        in_specs=[vmem] * 2,
        out_specs=(vmem,) * 4,
        scratch_shapes=[pltpu.VMEM((768, BLOCK), F32)],
        compiler_params=pltpu.CompilerParams(vmem_limit_bytes=VMEM_LIMIT),
        name="solve",
    )(gram, prod)


SPREAD_COPIES = 2 + 7 + 6 + 6 + 1


def spread_kernel(inv, side, prod, delta, part, dout, other, opart, dz, send_sems, recv_sems):
    me = Place()
    me.greet("xyzc")
    out = Sender(send_sems, recv_sems)
    x, y, z, c = me.x, me.y, me.z, me.c
    copies = [out.start(delta, other, me.partner()), out.start(part, opart, me.partner())]
    arrive(copies)
    cross = jnp.concatenate([opart[...], across(other[...], side[...])], axis=1)
    second = jnp.dot(prod[...] - cross, inv[...], precision=HI, preferred_element_type=F32)
    dz[z] = jnp.where(c == 0, delta[...], second)
    copies = []
    for d in range(1, NZ):
        copies.append(out.start(dz.at[z], dz.at[z], me.at_z(d)[1]))
    arrive(copies)
    dout[c, x, y] = dz[...].reshape(64, BLOCK).astype(BF16)
    copies = []
    for d in range(1, 4):
        copies.append(out.start(dout.at[c, x, y, 0:32], dout.at[c, x, y, 0:32], me.at_y(d)[1]))
        copies.append(out.start(dout.at[c, x, y, 32:64], dout.at[c, x, y, 32:64], me.at_x(d)[1]))
    arrive(copies)
    copies = []
    for d in range(1, 4):
        copies.append(out.start(dout.at[c, x, :, 0:32], dout.at[c, x, :, 0:32], me.at_x(d)[1]))
        copies.append(out.start(dout.at[c, :, y, 32:64], dout.at[c, :, y, 32:64], me.at_y(d)[1]))
    arrive(copies)
    arrive([out.start(dout.at[c], dout.at[c], me.partner())])
    out.drain()


def spread(inv, side, prod, delta, part):
    vmem = pl.BlockSpec(memory_space=pltpu.VMEM)
    return pl.pallas_call(
        spread_kernel,
        out_shape=jax.ShapeDtypeStruct((2, NX, NY, 64, BLOCK), BF16),
        in_specs=[vmem] * 5,
        out_specs=vmem,
        scratch_shapes=[
            pltpu.VMEM((8, BLOCK), F32),
            pltpu.VMEM((8, 256), F32),
            pltpu.VMEM((NZ, 8, BLOCK), F32),
            pltpu.SemaphoreType.DMA((SPREAD_COPIES,)),
            pltpu.SemaphoreType.DMA((SPREAD_COPIES,)),
        ],
        compiler_params=pltpu.CompilerParams(
            collective_id=2, has_side_effects=True, vmem_limit_bytes=VMEM_LIMIT
        ),
        name="spread",
    )(inv, side, prod, delta, part)


def unit_normalize(values):
    wide = values.astype(F32)
    scale = lax.rsqrt(jnp.mean(wide * wide, axis=1, keepdims=True) + 1e-06)
    return (wide * scale).astype(BF16)


def shards(features, labels, scores, landmarks, coefficients, block_ids):
    count = coefficients.shape[1]
    devices_all = lax.axis_size("rows") * lax.axis_size("rrep")
    ridge = float(features.shape[0] * devices_all)
    holder = lax.axis_index("rows")
    replica = lax.axis_index("rrep")
    xhat = unit_normalize(features)
    classes = jnp.arange(count, dtype=jnp.int32)
    residual = (labels[:, None] == classes[None, :]).astype(F32) - scores.astype(F32)
    rounded = jnp.pad(residual.astype(BF16), ((0, 0), (0, CLASSES - count)))
    share = landmarks.shape[0] // 8
    zslice = unit_normalize(lax.dynamic_slice_in_dim(landmarks, replica * share, share, 0))
    mine = (block_ids == holder)[:, None, None]
    zin = jnp.where(mine, zslice[None], jnp.zeros_like(zslice)[None])
    zin = zin.reshape(2, 4, 16, NY, 256).transpose(3, 0, 1, 2, 4).reshape(NY, NZ, 16, 256)
    zall, xp, rp = land(zin, xhat, rounded)
    kern, gram, prod = partials(zall, xhat, xp, rounded, rp)
    gram, prod = sums(gram, prod)
    inv, side, delta, part = solve(gram, prod, ridge)
    deltas = spread(inv, side, prod, delta, part).reshape(2, CLASSES, BLOCK)[:, :count]
    new_coefficients = coefficients
    for step in range(2):
        added = jnp.where(holder == block_ids[step], deltas[step].T.astype(F32), 0.0)
        new_coefficients = new_coefficients + added
        residual = residual - lax.dot_general(
            kern[:, step * BLOCK : (step + 1) * BLOCK],
            deltas[step],
            (((1,), (1,)), ((), ())),
            preferred_element_type=F32,
        )
    return (new_coefficients, residual)


def solution(mesh):
    in_specs = (
        P(("rows", "rrep"), None),
        P(("rows", "rrep")),
        P(("rows", "rrep"), None),
        P("rows", None),
        P("rows", None),
        P(),
    )
    out_specs = (P("rows", None), P(("rows", "rrep"), None))
    return jax.shard_map(shards, mesh=mesh, in_specs=in_specs, out_specs=out_specs, check_vma=False)
```

```python
import functools

import jax
import jax.numpy as jnp
from jax import lax
from jax.experimental import pallas as pl
from jax.experimental.pallas import tpu as pltpu
from jax.sharding import PartitionSpec as P

MESH = pl.DeviceIdType.MESH
HI = lax.Precision.HIGHEST
F32 = jnp.float32
BF16 = jnp.bfloat16
NX, NY, NZ = 4, 4, 8
BLOCK = 512
CLASSES = 1024
VMEM_LIMIT = 52 * 2**20
COPIES = 138
TILE = 128
TILES = BLOCK // TILE
BELOW = [(i, j) for i in range(TILES) for j in range(i)]
EXACT = dict(precision=HI, preferred_element_type=F32)


class Place:
    def __init__(self):
        rows, rrep = lax.axis_index("rows"), lax.axis_index("rrep")
        self.rows, self.rrep = rows, rrep
        self.y, self.z = rows // NZ, rows % NZ
        self.x, self.c = rrep // 2, rrep % 2

    def at_x(self, d):
        other = (self.x + d) % NX
        return other, (self.rows, other * 2 + self.c)

    def at_y(self, d):
        other = (self.y + d) % NY
        return other, (other * NZ + self.z, self.rrep)

    def at_z(self, d):
        other = (self.z + d) % NZ
        return other, (self.y * NZ + other, self.rrep)

    def partner(self):
        return (self.rows, self.x * 2 + 1 - self.c)

    def greet(self, axes):
        barrier = pltpu.get_barrier_semaphore()
        peers = []
        if "x" in axes:
            peers += [self.at_x(d)[1] for d in range(1, NX)]
        if "y" in axes:
            peers += [self.at_y(d)[1] for d in range(1, NY)]
        if "z" in axes:
            peers += [self.at_z(d)[1] for d in range(1, NZ)]
        if "c" in axes:
            peers += [self.partner()]
        for peer in peers:
            pl.semaphore_signal(barrier, inc=1, device_id=peer, device_id_type=MESH)
        pl.semaphore_wait(barrier, len(peers))


class Sender:
    def __init__(self, send_sems, recv_sems):
        self.send_sems, self.recv_sems = send_sems, recv_sems
        self.copies = []

    def start(self, src, dst, device):
        i = len(self.copies)
        copy = pltpu.make_async_remote_copy(
            src_ref=src,
            dst_ref=dst,
            send_sem=self.send_sems.at[i],
            recv_sem=self.recv_sems.at[i],
            device_id=device,
            device_id_type=MESH,
        )
        copy.start()
        self.copies.append(copy)
        return copy

    def drain(self):
        for copy in self.copies:
            copy.wait_send()


def arrive(copies):
    for copy in copies:
        copy.wait_recv()


def gather_landmarks(me, out, zin, xin, rin, zall, xp, rp, r1, s1, r2):
    x, y, z, c = me.x, me.y, me.z, me.c
    first = []
    for d in range(1, NY):
        other, device = me.at_y(d)
        first.append(out.start(zin.at[other], r1.at[d - 1], device))
    swap = [out.start(xin, xp, me.partner()), out.start(rin, rp, me.partner())]
    arrive(first)
    s1[...] = zin[y] + r1[0] + r1[1] + r1[2]
    second = []
    for d in range(1, NZ):
        other, device = me.at_z(d)
        second.append(out.start(s1.at[other], r2.at[d - 1], device))
    arrive(second)
    total = s1[z]
    for d in range(1, NZ):
        total = total + r2[d - 1]
    s, g = z // 4, z % 4
    zall[y, s, x, c, g] = total
    mine = zall.at[y, s, x, c, g]
    arrive([out.start(mine, mine, me.at_z(d)[1]) for d in range(1, NZ)])
    spread_plane(
        me,
        out,
        lambda i, j: zall.at[j, 0, i, c],
        lambda i, j: zall.at[j, 1, i, c],
        lambda i: zall.at[:, 0, i, c],
        lambda j: zall.at[j, 1, :, c],
    )
    arrive(swap)


def spread_plane(me, out, one_a, one_b, column, row):
    x, y = me.x, me.y
    copies = []
    for d in range(1, 4):
        copies.append(out.start(one_a(x, y), one_a(x, y), me.at_y(d)[1]))
        copies.append(out.start(one_b(x, y), one_b(x, y), me.at_x(d)[1]))
    arrive(copies)
    copies = []
    for d in range(1, 4):
        copies.append(out.start(column(x), column(x), me.at_x(d)[1]))
        copies.append(out.start(row(y), row(y), me.at_y(d)[1]))
    across = [
        out.start(column(x), column(x), me.partner()),
        out.start(row(y), row(y), me.partner()),
    ]
    for d in range(1, 4):
        arrive([copies[2 * d - 2]])
        source = (x - d) % NX
        across.append(out.start(column(source), column(source), me.partner()))
        arrive([copies[2 * d - 1]])
        source = (y - d) % NY
        across.append(out.start(row(source), row(source), me.partner()))
    arrive(across)


CONTRACT = (((0,), (0,)), ((), ()))


def columns_of(zall, xref, kern, start):
    rows = xref.shape[0]
    total = None
    for y in range(NY):
        part = lax.dot_general(
            xref[:, y * 256 : (y + 1) * 256],
            zall[y].reshape(2 * BLOCK, 256),
            (((1,), (1,)), ((), ())),
            preferred_element_type=F32,
        )
        total = part if total is None else total + part
    kern[start : start + rows, :] = jnp.exp(total * (1024**-0.5)).astype(BF16)


def eye_mask():
    rows = lax.broadcasted_iota(jnp.int32, (TILE, TILE), 0)
    cols = lax.broadcasted_iota(jnp.int32, (TILE, TILE), 1)
    return rows, cols


def partial_grams(me, kern, gin, diag):
    base = me.c * BLOCK
    rows, cols = eye_mask()
    diagonal = []
    for i in range(TILES):
        left = kern[:, pl.ds(pl.multiple_of(base + i * TILE, TILE), TILE)]
        right = kern[:, pl.ds(pl.multiple_of(base, TILE), (i + 1) * TILE)]
        panel = lax.dot_general(left, right, CONTRACT, preferred_element_type=F32)
        for j in range(i):
            k = BELOW.index((i, j))
            gin[k // NY, k % NY] = panel[:, j * TILE : (j + 1) * TILE].reshape(NZ, 16, TILE)
        diagonal.append(panel[:, i * TILE : (i + 1) * TILE])
    for k in range(2):
        both = jnp.where(rows >= cols, diagonal[2 * k], diagonal[2 * k + 1])
        gin[1, 2 + k] = both.reshape(NZ, 16, TILE)
        lost = jnp.where(rows == cols, diagonal[2 * k + 1], 0.0)
        diag[k : k + 1, :] = jnp.sum(lost, axis=0, keepdims=True)
    diag[2:, :] = jnp.zeros((6, TILE), F32)
    cross = kern[:, pl.ds(pl.multiple_of(BLOCK + me.c * 256, 256), 256)]
    side = lax.dot_general(cross, kern[:, :BLOCK], CONTRACT, preferred_element_type=F32)
    for i in range(2):
        for j in range(TILES):
            block = side[i * TILE : (i + 1) * TILE, j * TILE : (j + 1) * TILE]
            gin[2 + i, j] = block.reshape(NZ, 16, TILE)


def partial_products(me, kern, rin, rp, pin):
    rows = rin.shape[0]
    mine = pl.ds(pl.multiple_of(me.c * BLOCK, BLOCK), BLOCK)
    for x in range(NX):
        part = slice(x * 256, (x + 1) * 256)
        own = lax.dot_general(rin[:, part], kern[:rows, mine], CONTRACT, preferred_element_type=F32)
        other = lax.dot_general(rp[:, part], kern[rows:, mine], CONTRACT, preferred_element_type=F32)
        pin[x] = (own + other).reshape(NY, 64, BLOCK)


def sum_plane_one(me, out, src, ra, rb, h):
    copies = []
    for d in range(1, 4):
        i, device = me.at_x(d)
        copies.append(out.start(src.at[i, :, 0:h], ra.at[d - 1], device))
        i, device = me.at_y(d)
        copies.append(out.start(src.at[:, i, h : 2 * h], rb.at[d - 1], device))
    return copies


def sum_plane_two(me, out, sa, sb, ra, rb):
    copies = []
    for d in range(1, 4):
        i, device = me.at_y(d)
        copies.append(out.start(sa.at[i], ra.at[d - 1], device))
        i, device = me.at_x(d)
        copies.append(out.start(sb.at[i], rb.at[d - 1], device))
    return copies


def sum_line(me, out, src, received):
    copies = []
    for d in range(1, NZ):
        i, device = me.at_z(d)
        copies.append(out.start(src.at[i], received.at[d - 1], device))
    return copies


def total_of(own, received):
    for d in range(received.shape[0]):
        own = own + received[d]
    return own


def eliminate_rows(values, k, n):
    lane = lax.broadcasted_iota(jnp.int32, (8, n), 1)
    sub = lax.broadcasted_iota(jnp.int32, (8, n), 0)
    rows = values[k : k + 8, :]
    pivots = [jnp.broadcast_to(rows[:, k + q : k + q + 1], (8, n)) for q in range(8)]
    inside = (lane >= k) & (lane < k + 8)
    panel = jnp.where(inside, (lane - k == sub).astype(F32), rows)
    for q in range(8):
        factor = pivots[q]
        inverse = 1.0 / jnp.broadcast_to(factor[q : q + 1, :], (8, n))
        own = sub == q

        def update(block):
            row = jnp.broadcast_to(block[q : q + 1, :], (8, n)) * inverse
            return jnp.where(own, row, block - factor * row)

        for j in range(q + 1, 8):
            pivots[j] = update(pivots[j])
        panel = update(panel)
    return panel


def invert_tile(values, n):
    lane = lax.broadcasted_iota(jnp.int32, (n, n), 1)
    for k in range(0, n, 8):
        panel = eliminate_rows(values, k, n)
        inside = (lane >= k) & (lane < k + 8)
        rest = jnp.where(inside, 0.0, values)
        for q in range(8):
            column = jnp.broadcast_to(values[:, k + q : k + q + 1], (n, n))
            rest = rest - column * jnp.broadcast_to(panel[q : q + 1, :], (n, n))
        parts = ([rest[:k]] if k else []) + [panel] + ([rest[k + 8 :]] if k + 8 < n else [])
        values = jnp.concatenate(parts, axis=0)
    return values


def invert_step(ref, j):
    s = slice(j * TILE, (j + 1) * TILE)
    inverse = invert_tile(ref[s, s], TILE)
    row = jnp.dot(inverse, ref[s, :], **EXACT)
    column = ref[:, s]
    ref[:, s] = jnp.zeros((BLOCK, TILE), F32)
    parts = ([row[:, : j * TILE]] if j else []) + [inverse]
    parts += [row[:, (j + 1) * TILE :]] if j < TILES - 1 else []
    row = jnp.concatenate(parts, axis=1)
    for i in range(TILES):
        t = slice(i * TILE, (i + 1) * TILE)
        if i != j:
            ref[t, :] -= jnp.dot(column[t], row, **EXACT)
    ref[s, :] = row


def unpack_grams(ridge, gall, diag, inv, side):
    rows, cols = eye_mask()
    for k, (i, j) in enumerate(BELOW):
        block = gall[k // NY, k % NY].reshape(TILE, TILE)
        inv[i * TILE : (i + 1) * TILE, j * TILE : (j + 1) * TILE] = block
        inv[j * TILE : (j + 1) * TILE, i * TILE : (i + 1) * TILE] = block.T
    for k in range(2):
        both = gall[1, 2 + k].reshape(TILE, TILE)
        turned = both.T
        lower = jnp.where(rows >= cols, both, turned)
        upper = jnp.where(rows < cols, both, turned)
        upper = jnp.where(rows == cols, diag[k : k + 1, :], upper)
        for i, block in ((2 * k, lower), (2 * k + 1, upper)):
            s = slice(i * TILE, (i + 1) * TILE)
            inv[s, s] = block + jnp.where(rows == cols, ridge, 0.0)
    for i in range(2):
        for j in range(TILES):
            side[i * TILE : (i + 1) * TILE, j * TILE : (j + 1) * TILE] = gall[2 + i, j].reshape(TILE, TILE)


def cross_product(delta, side):
    return lax.dot_general(delta.astype(BF16).astype(F32), side, (((1,), (1,)), ((), ())), **EXACT)


def update_kernel(
    ridge,
    zin, xin, rin,
    kout, dout,
    zall, xp, rp, r1, s1, r2,
    kern, gin, diag, pin,
    ga1, gb1, ga, gb, ga2, gb2, g2, g3, gall,
    dx, dxs, dy, dys, dz,
    pa1, pb1, pa, pb, pa2, pb2, p2, p3, prod,
    inv, side, delta, part, other, opart,
    send_sems, recv_sems,
):
    me = Place()
    me.greet("xyzc")
    out = Sender(send_sems, recv_sems)
    x, y, z, c = me.x, me.y, me.z, me.c
    rows = xin.shape[0]
    gather_landmarks(me, out, zin, xin, rin, zall, xp, rp, r1, s1, r2)
    columns_of(zall, xin, kern, 0)
    columns_of(zall, xp, kern, rows)
    partial_grams(me, kern, gin, diag)

    grams = sum_plane_one(me, out, gin, ga1, gb1, 4)
    diags = [out.start(diag, dx.at[d - 1], me.at_x(d)[1]) for d in range(1, NX)]
    kout[...] = kern[:rows, :]
    partial_products(me, kern, rin, rp, pin)
    arrive(grams)
    ga[...] = total_of(gin[x, :, 0:4], ga1)
    gb[...] = total_of(gin[:, y, 4:8], gb1)
    grams = sum_plane_two(me, out, ga, gb, ga2, gb2)
    arrive(diags)
    dxs[...] = total_of(diag[...], dx)
    diags = [out.start(dxs, dy.at[d - 1], me.at_y(d)[1]) for d in range(1, NY)]
    arrive(grams)
    g2[0:4] = total_of(ga[y], ga2)
    g2[4:8] = total_of(gb[x], gb2)
    grams = sum_line(me, out, g2, g3)
    products = sum_plane_one(me, out, pin, pa1, pb1, 32)
    arrive(diags)
    dys[...] = total_of(dxs[...], dy)
    diags = [out.start(dys, dz.at[d - 1], me.at_z(d)[1]) for d in range(1, NZ)]
    arrive(grams)
    gall[x, y, z] = total_of(g2[z], g3)
    mine = gall.at[x, y, z]
    grams = [out.start(mine, mine, me.at_z(d)[1]) for d in range(1, NZ)]
    arrive(grams)
    grams = []
    for d in range(1, 4):
        grams.append(out.start(gall.at[x, y, 0:4], gall.at[x, y, 0:4], me.at_y(d)[1]))
        grams.append(out.start(gall.at[x, y, 4:8], gall.at[x, y, 4:8], me.at_x(d)[1]))
    arrive(products)
    pa[...] = total_of(pin[x, :, 0:32], pa1)
    pb[...] = total_of(pin[:, y, 32:64], pb1)
    arrive(grams)
    grams = []
    for d in range(1, 4):
        grams.append(out.start(gall.at[x, :, 0:4], gall.at[x, :, 0:4], me.at_x(d)[1]))
        grams.append(out.start(gall.at[:, y, 4:8], gall.at[:, y, 4:8], me.at_y(d)[1]))
    products = sum_plane_two(me, out, pa, pb, pa2, pb2)
    arrive(diags)
    lost = total_of(dys[...], dz)
    arrive(grams)

    unpack_grams(ridge, gall, lost, inv, side)
    invert_step(inv, 0)
    arrive(products)
    p2[0:4] = total_of(pa[y], pa2).reshape(4, 8, BLOCK)
    p2[4:8] = total_of(pb[x], pb2).reshape(4, 8, BLOCK)
    products = sum_line(me, out, p2, p3)
    invert_step(inv, 1)
    invert_step(inv, 2)
    arrive(products)
    prod[z] = total_of(p2[z], p3)
    products = [out.start(prod.at[z], prod.at[z], me.at_z(d)[1]) for d in range(1, NZ)]
    invert_step(inv, 3)
    arrive(products)

    target = prod[...].reshape(64, BLOCK)
    first = jnp.dot(target, inv[...], **EXACT)
    delta[...] = first
    swap = [out.start(delta, other, me.partner())]
    part[...] = cross_product(first, side[...])
    swap.append(out.start(part, opart, me.partner()))
    arrive(swap[:1])
    here = cross_product(other[...], side[...])
    arrive(swap[1:])
    cross = jnp.concatenate([opart[...], here], axis=1)
    second = jnp.dot(target - cross, inv[...], **EXACT)
    dout[c, x, y] = jnp.where(c == 0, first, second).astype(BF16)
    spread_plane(
        me,
        out,
        lambda i, j: dout.at[c, i, j, 0:32],
        lambda i, j: dout.at[c, i, j, 32:64],
        lambda i: dout.at[c, i, :, 0:32],
        lambda j: dout.at[c, :, j, 32:64],
    )
    out.drain()


def update(zin, xhat, rounded, ridge):
    rows = xhat.shape[0]
    vmem = pl.BlockSpec(memory_space=pltpu.VMEM)
    wide = lambda *shape: pltpu.VMEM(shape, F32)
    half = lambda *shape: pltpu.VMEM(shape, BF16)
    return pl.pallas_call(
        functools.partial(update_kernel, ridge),
        out_shape=(
            jax.ShapeDtypeStruct((rows, 2 * BLOCK), BF16),
            jax.ShapeDtypeStruct((2, NX, NY, 64, BLOCK), BF16),
        ),
        in_specs=[vmem] * 3,
        out_specs=(vmem,) * 2,
        scratch_shapes=[
            half(NY, 2, NX, 2, 4, 16, 256),
            half(rows, 1024),
            half(rows, CLASSES),
            half(NY - 1, NZ, 16, 256),
            half(NZ, 16, 256),
            half(NZ - 1, 16, 256),
            half(2 * rows, 2 * BLOCK),
            wide(NX, NY, NZ, 16, TILE),
            wide(8, TILE),
            wide(NX, NY, 64, BLOCK),
            wide(3, 4, 4, 16, TILE),
            wide(3, 4, 4, 16, TILE),
            wide(4, 4, 16, TILE),
            wide(4, 4, 16, TILE),
            wide(3, 4, 16, TILE),
            wide(3, 4, 16, TILE),
            wide(NZ, 16, TILE),
            wide(NZ - 1, 16, TILE),
            wide(NX, NY, NZ, 16, TILE),
            wide(3, 8, TILE),
            wide(8, TILE),
            wide(3, 8, TILE),
            wide(8, TILE),
            wide(NZ - 1, 8, TILE),
            wide(3, 4, 32, BLOCK),
            wide(3, 4, 32, BLOCK),
            wide(4, 32, BLOCK),
            wide(4, 32, BLOCK),
            wide(3, 32, BLOCK),
            wide(3, 32, BLOCK),
            wide(NZ, 8, BLOCK),
            wide(NZ - 1, 8, BLOCK),
            wide(NZ, 8, BLOCK),
            wide(BLOCK, BLOCK),
            wide(256, BLOCK),
            wide(64, BLOCK),
            wide(64, 256),
            wide(64, BLOCK),
            wide(64, 256),
            pltpu.SemaphoreType.DMA((COPIES,)),
            pltpu.SemaphoreType.DMA((COPIES,)),
        ],
        compiler_params=pltpu.CompilerParams(
            collective_id=0, has_side_effects=True, vmem_limit_bytes=VMEM_LIMIT
        ),
        name="update",
    )(zin, xhat, rounded)


def unit_normalize(values):
    wide = values.astype(F32)
    scale = lax.rsqrt(jnp.mean(wide * wide, axis=1, keepdims=True) + 1e-06)
    return (wide * scale).astype(BF16)


def shards(features, labels, scores, landmarks, coefficients, block_ids):
    count = coefficients.shape[1]
    devices_all = lax.axis_size("rows") * lax.axis_size("rrep")
    ridge = float(features.shape[0] * devices_all)
    holder = lax.axis_index("rows")
    replica = lax.axis_index("rrep")
    xhat = unit_normalize(features)
    classes = jnp.arange(count, dtype=jnp.int32)
    residual = (labels[:, None] == classes[None, :]).astype(F32) - scores.astype(F32)
    rounded = jnp.pad(residual.astype(BF16), ((0, 0), (0, CLASSES - count)))
    share = landmarks.shape[0] // 8
    zslice = unit_normalize(lax.dynamic_slice_in_dim(landmarks, replica * share, share, 0))
    mine = (block_ids == holder)[:, None, None]
    zin = jnp.where(mine, zslice[None], jnp.zeros_like(zslice)[None])
    zin = zin.reshape(2, 4, 16, NY, 256).transpose(3, 0, 1, 2, 4).reshape(NY, NZ, 16, 256)
    kern, deltas = update(zin, xhat, rounded, ridge)
    deltas = deltas.reshape(2, CLASSES, BLOCK)[:, :count]
    new_coefficients = coefficients
    for step in range(2):
        added = jnp.where(holder == block_ids[step], deltas[step].T.astype(F32), 0.0)
        new_coefficients = new_coefficients + added
        residual = residual - lax.dot_general(
            kern[:, step * BLOCK : (step + 1) * BLOCK],
            deltas[step],
            (((1,), (1,)), ((), ())),
            preferred_element_type=F32,
        )
    return (new_coefficients, residual)


def solution(mesh):
    in_specs = (
        P(("rows", "rrep"), None),
        P(("rows", "rrep")),
        P(("rows", "rrep"), None),
        P("rows", None),
        P("rows", None),
        P(),
    )
    out_specs = (P("rows", None), P(("rows", "rrep"), None))
    return jax.shard_map(shards, mesh=mesh, in_specs=in_specs, out_specs=out_specs, check_vma=False)
```

```python
import functools

import jax
import jax.numpy as jnp
from jax import lax
from jax.experimental import pallas as pl
from jax.experimental.pallas import tpu as pltpu
from jax.sharding import PartitionSpec as P

MESH = pl.DeviceIdType.MESH
HI = lax.Precision.HIGHEST
F32 = jnp.float32
BF16 = jnp.bfloat16
NX, NY, NZ = 4, 4, 8
BLOCK = 512
CLASSES = 1024
VMEM_LIMIT = 52 * 2**20
COPIES = 138
TILE = 128
TILES = BLOCK // TILE
BELOW = [(i, j) for i in range(TILES) for j in range(i)]
EXACT = dict(precision=HI, preferred_element_type=F32)


class Place:
    def __init__(self):
        rows, rrep = lax.axis_index("rows"), lax.axis_index("rrep")
        self.rows, self.rrep = rows, rrep
        self.y, self.z = rows // NZ, rows % NZ
        self.x, self.c = rrep // 2, rrep % 2

    def at_x(self, d):
        other = (self.x + d) % NX
        return other, (self.rows, other * 2 + self.c)

    def at_y(self, d):
        other = (self.y + d) % NY
        return other, (other * NZ + self.z, self.rrep)

    def at_z(self, d):
        other = (self.z + d) % NZ
        return other, (self.y * NZ + other, self.rrep)

    def partner(self):
        return (self.rows, self.x * 2 + 1 - self.c)

    def greet(self, axes):
        barrier = pltpu.get_barrier_semaphore()
        peers = []
        if "x" in axes:
            peers += [self.at_x(d)[1] for d in range(1, NX)]
        if "y" in axes:
            peers += [self.at_y(d)[1] for d in range(1, NY)]
        if "z" in axes:
            peers += [self.at_z(d)[1] for d in range(1, NZ)]
        if "c" in axes:
            peers += [self.partner()]
        for peer in peers:
            pl.semaphore_signal(barrier, inc=1, device_id=peer, device_id_type=MESH)
        pl.semaphore_wait(barrier, len(peers))


class Sender:
    def __init__(self, send_sems, recv_sems):
        self.send_sems, self.recv_sems = send_sems, recv_sems
        self.copies = []

    def make(self, src, dst, device):
        i = len(self.copies)
        copy = pltpu.make_async_remote_copy(
            src_ref=src,
            dst_ref=dst,
            send_sem=self.send_sems.at[i],
            recv_sem=self.recv_sems.at[i],
            device_id=device,
            device_id_type=MESH,
        )
        self.copies.append(copy)
        return copy

    def start(self, src, dst, device):
        copy = self.make(src, dst, device)
        copy.start()
        return copy

    def drain(self):
        for copy in self.copies:
            copy.wait_send()


def arrive(copies):
    for copy in copies:
        copy.wait_recv()


def unit_normalize(values):
    wide = values.astype(F32)
    scale = lax.rsqrt(jnp.mean(wide * wide, axis=1, keepdims=True) + 1e-06)
    return (wide * scale).astype(BF16)


def masked_landmarks(me, block_ids, lands, zin):
    share = unit_normalize(lands[...])
    for s in range(2):
        held = jnp.where(block_ids[s] == me.rows, 1.0, 0.0).astype(BF16)
        kept = share * held
        for y in range(NY):
            for g in range(4):
                zin[y, s * 4 + g] = kept[g * 16 : (g + 1) * 16, y * 256 : (y + 1) * 256]


def own_rows(features, labels, scores, xin, rin):
    count = scores.shape[1]
    xin[...] = unit_normalize(features[...])
    classes = lax.broadcasted_iota(jnp.int32, scores.shape, 1)
    target = jnp.where(classes == labels[...], 1.0, 0.0)
    rin[:, CLASSES - 128 :] = jnp.zeros((rin.shape[0], 128), BF16)
    rin[:, :count] = (target - scores[...].astype(F32)).astype(BF16)


def gather_landmarks(me, out, zin, rows, fetches, xin, rin, zall, xp, rp, r1, s1, r2):
    x, y, z, c = me.x, me.y, me.z, me.c
    first = []
    for d in range(1, NY):
        other, device = me.at_y(d)
        first.append(out.start(zin.at[other], r1.at[d - 1], device))
    for fetch in fetches:
        fetch.wait()
    own_rows(*rows, xin, rin)
    swap = [out.start(xin, xp, me.partner()), out.start(rin, rp, me.partner())]
    arrive(first)
    s1[...] = zin[y] + r1[0] + r1[1] + r1[2]
    second = []
    for d in range(1, NZ):
        other, device = me.at_z(d)
        second.append(out.start(s1.at[other], r2.at[d - 1], device))
    arrive(second)
    total = s1[z]
    for d in range(1, NZ):
        total = total + r2[d - 1]
    s, g = z // 4, z % 4
    zall[y, s, x, c, g] = total
    mine = zall.at[y, s, x, c, g]
    arrive([out.start(mine, mine, me.at_z(d)[1]) for d in range(1, NZ)])
    spread_plane(
        me,
        out,
        lambda i, j: zall.at[j, 0, i, c],
        lambda i, j: zall.at[j, 1, i, c],
        lambda i: zall.at[:, 0, i, c],
        lambda j: zall.at[j, 1, :, c],
    )
    arrive(swap)


def spread_plane(me, out, one_a, one_b, column, row):
    x, y = me.x, me.y
    copies = []
    for d in range(1, 4):
        copies.append(out.start(one_a(x, y), one_a(x, y), me.at_y(d)[1]))
        copies.append(out.start(one_b(x, y), one_b(x, y), me.at_x(d)[1]))
    arrive(copies)
    copies = []
    for d in range(1, 4):
        copies.append(out.start(column(x), column(x), me.at_x(d)[1]))
        copies.append(out.start(row(y), row(y), me.at_y(d)[1]))
    across = [
        out.start(column(x), column(x), me.partner()),
        out.start(row(y), row(y), me.partner()),
    ]
    for d in range(1, 4):
        arrive([copies[2 * d - 2]])
        source = (x - d) % NX
        across.append(out.start(column(source), column(source), me.partner()))
        arrive([copies[2 * d - 1]])
        source = (y - d) % NY
        across.append(out.start(row(source), row(source), me.partner()))
    arrive(across)


CONTRACT = (((0,), (0,)), ((), ()))


def columns_of(zall, xref, kern, start):
    rows = xref.shape[0]
    total = None
    for y in range(NY):
        part = lax.dot_general(
            xref[:, y * 256 : (y + 1) * 256],
            zall[y].reshape(2 * BLOCK, 256),
            (((1,), (1,)), ((), ())),
            preferred_element_type=F32,
        )
        total = part if total is None else total + part
    kern[start : start + rows, :] = jnp.exp(total * (1024**-0.5)).astype(BF16)


def eye_mask():
    rows = lax.broadcasted_iota(jnp.int32, (TILE, TILE), 0)
    cols = lax.broadcasted_iota(jnp.int32, (TILE, TILE), 1)
    return rows, cols


def partial_grams(me, kern, gin, diag):
    base = me.c * BLOCK
    rows, cols = eye_mask()
    diagonal = []
    for i in range(TILES):
        left = kern[:, pl.ds(pl.multiple_of(base + i * TILE, TILE), TILE)]
        right = kern[:, pl.ds(pl.multiple_of(base, TILE), (i + 1) * TILE)]
        panel = lax.dot_general(left, right, CONTRACT, preferred_element_type=F32)
        for j in range(i):
            k = BELOW.index((i, j))
            gin[k // NY, k % NY] = panel[:, j * TILE : (j + 1) * TILE].reshape(NZ, 16, TILE)
        diagonal.append(panel[:, i * TILE : (i + 1) * TILE])
    for k in range(2):
        both = jnp.where(rows >= cols, diagonal[2 * k], diagonal[2 * k + 1])
        gin[1, 2 + k] = both.reshape(NZ, 16, TILE)
        lost = jnp.where(rows == cols, diagonal[2 * k + 1], 0.0)
        diag[k : k + 1, :] = jnp.sum(lost, axis=0, keepdims=True)
    diag[2:, :] = jnp.zeros((6, TILE), F32)
    cross = kern[:, pl.ds(pl.multiple_of(BLOCK + me.c * 256, 256), 256)]
    side = lax.dot_general(cross, kern[:, :BLOCK], CONTRACT, preferred_element_type=F32)
    for i in range(2):
        for j in range(TILES):
            block = side[i * TILE : (i + 1) * TILE, j * TILE : (j + 1) * TILE]
            gin[2 + i, j] = block.reshape(NZ, 16, TILE)


def partial_products(me, kern, rin, rp, pin):
    rows = rin.shape[0]
    mine = pl.ds(pl.multiple_of(me.c * BLOCK, BLOCK), BLOCK)

    def step(x, carry):
        part = pl.ds(pl.multiple_of(x * 256, 256), 256)
        own = lax.dot_general(rin[:, part], kern[:rows, mine], CONTRACT, preferred_element_type=F32)
        other = lax.dot_general(rp[:, part], kern[rows:, mine], CONTRACT, preferred_element_type=F32)
        pin[x] = (own + other).reshape(NY, 64, BLOCK)
        return carry

    lax.fori_loop(0, NX, step, 0)


def sum_plane_one(me, out, src, ra, rb, h):
    copies = []
    for d in range(1, 4):
        i, device = me.at_x(d)
        copies.append(out.start(src.at[i, :, 0:h], ra.at[d - 1], device))
        i, device = me.at_y(d)
        copies.append(out.start(src.at[:, i, h : 2 * h], rb.at[d - 1], device))
    return copies


def sum_plane_two(me, out, sa, sb, ra, rb):
    copies = []
    for d in range(1, 4):
        i, device = me.at_y(d)
        copies.append(out.start(sa.at[i], ra.at[d - 1], device))
        i, device = me.at_x(d)
        copies.append(out.start(sb.at[i], rb.at[d - 1], device))
    return copies


def sum_line(me, out, src, received):
    copies = []
    for d in range(1, NZ):
        i, device = me.at_z(d)
        copies.append(out.start(src.at[i], received.at[d - 1], device))
    return copies


def total_of(own, received):
    for d in range(received.shape[0]):
        own = own + received[d]
    return own


def eliminate_rows(values, k, n):
    lane = lax.broadcasted_iota(jnp.int32, (8, n), 1)
    sub = lax.broadcasted_iota(jnp.int32, (8, n), 0)
    rows = values[k : k + 8, :]
    pivots = [jnp.broadcast_to(rows[:, k + q : k + q + 1], (8, n)) for q in range(8)]
    inside = (lane >= k) & (lane < k + 8)
    panel = jnp.where(inside, (lane - k == sub).astype(F32), rows)
    for q in range(8):
        factor = pivots[q]
        inverse = 1.0 / jnp.broadcast_to(factor[q : q + 1, :], (8, n))
        own = sub == q

        def update(block):
            row = jnp.broadcast_to(block[q : q + 1, :], (8, n)) * inverse
            return jnp.where(own, row, block - factor * row)

        for j in range(q + 1, 8):
            pivots[j] = update(pivots[j])
        panel = update(panel)
    return panel


def invert_tile(values, n):
    lane = lax.broadcasted_iota(jnp.int32, (n, n), 1)
    for k in range(0, n, 8):
        panel = eliminate_rows(values, k, n)
        inside = (lane >= k) & (lane < k + 8)
        rest = jnp.where(inside, 0.0, values)
        for q in range(8):
            column = jnp.broadcast_to(values[:, k + q : k + q + 1], (n, n))
            rest = rest - column * jnp.broadcast_to(panel[q : q + 1, :], (n, n))
        parts = ([rest[:k]] if k else []) + [panel] + ([rest[k + 8 :]] if k + 8 < n else [])
        values = jnp.concatenate(parts, axis=0)
    return values


def invert(ref, row, halfway):
    def step(j, carry):
        pl.when(j == TILES // 2)(halfway)
        s = pl.ds(pl.multiple_of(j * TILE, TILE), TILE)
        inverse = invert_tile(ref[s, s], TILE)
        row[...] = jnp.dot(inverse, ref[s, :], **EXACT)
        row[:, s] = inverse
        column = ref[:, s]
        ref[:, s] = jnp.zeros((BLOCK, TILE), F32)
        for i in range(TILES):
            t = slice(i * TILE, (i + 1) * TILE)
            ref[t, :] -= jnp.dot(column[t], row[...], **EXACT)
        ref[s, :] = row[...]
        return carry

    lax.fori_loop(0, TILES, step, 0)


def unpack_grams(ridge, gall, diag, inv, side):
    rows, cols = eye_mask()
    for k, (i, j) in enumerate(BELOW):
        block = gall[k // NY, k % NY].reshape(TILE, TILE)
        inv[i * TILE : (i + 1) * TILE, j * TILE : (j + 1) * TILE] = block
        inv[j * TILE : (j + 1) * TILE, i * TILE : (i + 1) * TILE] = block.T
    for k in range(2):
        both = gall[1, 2 + k].reshape(TILE, TILE)
        turned = both.T
        lower = jnp.where(rows >= cols, both, turned)
        upper = jnp.where(rows < cols, both, turned)
        upper = jnp.where(rows == cols, diag[k : k + 1, :], upper)
        for i, block in ((2 * k, lower), (2 * k + 1, upper)):
            s = slice(i * TILE, (i + 1) * TILE)
            inv[s, s] = block + jnp.where(rows == cols, ridge, 0.0)
    for i in range(2):
        for j in range(TILES):
            side[i * TILE : (i + 1) * TILE, j * TILE : (j + 1) * TILE] = gall[2 + i, j].reshape(TILE, TILE)


def cross_product(delta, side):
    return lax.dot_general(delta.astype(BF16).astype(F32), side, (((1,), (1,)), ((), ())), **EXACT)


def update_kernel(
    ridge,
    block_ids, lands_all, features_all, labels_all, scores_all,
    kout, dout,
    lands, features, labels, scores, fetch_sems, zin, xin, rin, zall, xp, rp, r1, s1, r2,
    kern, gin, diag, pin,
    ga1, gb1, ga, gb, ga2, gb2, g2, g3, gall,
    dx, dxs, dy, dys, dz,
    pa1, pb1, pa, pb, pa2, pb2, p2, p3, prod,
    inv, pivots, side, delta, part, other, opart,
    send_sems, recv_sems,
):
    me = Place()
    share = lands.shape[0]
    start = pl.multiple_of(me.rrep * share, share)
    fetches = [
        pltpu.make_async_copy(src, dst, fetch_sems.at[i])
        for i, (src, dst) in enumerate(
            (
                (lands_all.at[pl.ds(start, share)], lands),
                (features_all, features),
                (labels_all, labels),
                (scores_all, scores),
            )
        )
    ]
    for fetch in fetches:
        fetch.start()
    fetches[0].wait()
    masked_landmarks(me, block_ids, lands, zin)
    me.greet("xyzc")
    out = Sender(send_sems, recv_sems)
    x, y, z, c = me.x, me.y, me.z, me.c
    rows = xin.shape[0]
    gather_landmarks(me, out, zin, (features, labels, scores), fetches[1:], xin, rin, zall, xp, rp, r1, s1, r2)
    columns_of(zall, xin, kern, 0)
    columns_of(zall, xp, kern, rows)
    partial_grams(me, kern, gin, diag)

    grams = sum_plane_one(me, out, gin, ga1, gb1, 4)
    diags = [out.start(diag, dx.at[d - 1], me.at_x(d)[1]) for d in range(1, NX)]
    kout[...] = kern[:rows, :]
    partial_products(me, kern, rin, rp, pin)
    arrive(grams)
    ga[...] = total_of(gin[x, :, 0:4], ga1)
    gb[...] = total_of(gin[:, y, 4:8], gb1)
    grams = sum_plane_two(me, out, ga, gb, ga2, gb2)
    arrive(diags)
    dxs[...] = total_of(diag[...], dx)
    diags = [out.start(dxs, dy.at[d - 1], me.at_y(d)[1]) for d in range(1, NY)]
    arrive(grams)
    g2[0:4] = total_of(ga[y], ga2)
    g2[4:8] = total_of(gb[x], gb2)
    grams = sum_line(me, out, g2, g3)
    products = sum_plane_one(me, out, pin, pa1, pb1, 32)
    arrive(diags)
    dys[...] = total_of(dxs[...], dy)
    diags = [out.start(dys, dz.at[d - 1], me.at_z(d)[1]) for d in range(1, NZ)]
    arrive(grams)
    gall[x, y, z] = total_of(g2[z], g3)
    mine = gall.at[x, y, z]
    grams = [out.start(mine, mine, me.at_z(d)[1]) for d in range(1, NZ)]
    arrive(grams)
    grams = []
    for d in range(1, 4):
        grams.append(out.start(gall.at[x, y, 0:4], gall.at[x, y, 0:4], me.at_y(d)[1]))
        grams.append(out.start(gall.at[x, y, 4:8], gall.at[x, y, 4:8], me.at_x(d)[1]))
    arrive(products)
    pa[...] = total_of(pin[x, :, 0:32], pa1)
    pb[...] = total_of(pin[:, y, 32:64], pb1)
    arrive(grams)
    grams = []
    for d in range(1, 4):
        grams.append(out.start(gall.at[x, :, 0:4], gall.at[x, :, 0:4], me.at_x(d)[1]))
        grams.append(out.start(gall.at[:, y, 4:8], gall.at[:, y, 4:8], me.at_y(d)[1]))
    products = sum_plane_two(me, out, pa, pb, pa2, pb2)
    arrive(diags)
    lost = total_of(dys[...], dz)
    arrive(grams)

    unpack_grams(ridge, gall, lost, inv, side)
    arrive(products)
    p2[0:4] = total_of(pa[y], pa2).reshape(4, 8, BLOCK)
    p2[4:8] = total_of(pb[x], pb2).reshape(4, 8, BLOCK)
    products = sum_line(me, out, p2, p3)
    returns = [out.make(prod.at[z], prod.at[z], me.at_z(d)[1]) for d in range(1, NZ)]

    def halfway():
        arrive(products)
        prod[z] = total_of(p2[z], p3)
        for copy in returns:
            copy.start()

    invert(inv, pivots, halfway)
    arrive(returns)

    target = prod[...].reshape(64, BLOCK)
    first = jnp.dot(target, inv[...], **EXACT)
    delta[...] = first
    swap = [out.start(delta, other, me.partner())]
    part[...] = cross_product(first, side[...])
    swap.append(out.start(part, opart, me.partner()))
    arrive(swap[:1])
    here = cross_product(other[...], side[...])
    arrive(swap[1:])
    cross = jnp.concatenate([opart[...], here], axis=1)
    second = jnp.dot(target - cross, inv[...], **EXACT)
    dout[c, x, y] = jnp.where(c == 0, first, second).astype(BF16)
    spread_plane(
        me,
        out,
        lambda i, j: dout.at[c, i, j, 0:32],
        lambda i, j: dout.at[c, i, j, 32:64],
        lambda i: dout.at[c, i, :, 0:32],
        lambda j: dout.at[c, :, j, 32:64],
    )
    out.drain()


def update(block_ids, landmarks, features, labels, scores, ridge):
    rows = features.shape[0]
    share = landmarks.shape[0] // 8
    vmem = pl.BlockSpec(memory_space=pltpu.VMEM)
    wide = lambda *shape: pltpu.VMEM(shape, F32)
    half = lambda *shape: pltpu.VMEM(shape, BF16)
    return pl.pallas_call(
        functools.partial(update_kernel, ridge),
        out_shape=(
            jax.ShapeDtypeStruct((rows, 2 * BLOCK), BF16),
            jax.ShapeDtypeStruct((2, NX, NY, 64, BLOCK), BF16),
        ),
        in_specs=[pl.BlockSpec(memory_space=pltpu.SMEM)] + [pl.BlockSpec(memory_space=pl.ANY)] * 4,
        out_specs=(vmem,) * 2,
        scratch_shapes=[
            half(share, 1024),
            half(rows, 1024),
            pltpu.VMEM((rows, 1), jnp.int32),
            half(rows, scores.shape[1]),
            pltpu.SemaphoreType.DMA((4,)),
            half(NY, NZ, 16, 256),
            half(rows, 1024),
            half(rows, CLASSES),
            half(NY, 2, NX, 2, 4, 16, 256),
            half(rows, 1024),
            half(rows, CLASSES),
            half(NY - 1, NZ, 16, 256),
            half(NZ, 16, 256),
            half(NZ - 1, 16, 256),
            half(2 * rows, 2 * BLOCK),
            wide(NX, NY, NZ, 16, TILE),
            wide(8, TILE),
            wide(NX, NY, 64, BLOCK),
            wide(3, 4, 4, 16, TILE),
            wide(3, 4, 4, 16, TILE),
            wide(4, 4, 16, TILE),
            wide(4, 4, 16, TILE),
            wide(3, 4, 16, TILE),
            wide(3, 4, 16, TILE),
            wide(NZ, 16, TILE),
            wide(NZ - 1, 16, TILE),
            wide(NX, NY, NZ, 16, TILE),
            wide(3, 8, TILE),
            wide(8, TILE),
            wide(3, 8, TILE),
            wide(8, TILE),
            wide(NZ - 1, 8, TILE),
            wide(3, 4, 32, BLOCK),
            wide(3, 4, 32, BLOCK),
            wide(4, 32, BLOCK),
            wide(4, 32, BLOCK),
            wide(3, 32, BLOCK),
            wide(3, 32, BLOCK),
            wide(NZ, 8, BLOCK),
            wide(NZ - 1, 8, BLOCK),
            wide(NZ, 8, BLOCK),
            wide(BLOCK, BLOCK),
            wide(TILE, BLOCK),
            wide(256, BLOCK),
            wide(64, BLOCK),
            wide(64, 256),
            wide(64, BLOCK),
            wide(64, 256),
            pltpu.SemaphoreType.DMA((COPIES,)),
            pltpu.SemaphoreType.DMA((COPIES,)),
        ],
        compiler_params=pltpu.CompilerParams(
            collective_id=0, has_side_effects=True, vmem_limit_bytes=VMEM_LIMIT
        ),
        name="update",
    )(block_ids, landmarks, features, labels, scores)


def shards(features, labels, scores, landmarks, coefficients, block_ids):
    count = coefficients.shape[1]
    devices_all = lax.axis_size("rows") * lax.axis_size("rrep")
    ridge = float(features.shape[0] * devices_all)
    holder = lax.axis_index("rows")
    classes = jnp.arange(count, dtype=jnp.int32)
    residual = (labels[:, None] == classes[None, :]).astype(F32) - scores.astype(F32)
    kern, deltas = update(block_ids, landmarks, features, labels[:, None], scores, ridge)
    deltas = deltas.reshape(2, CLASSES, BLOCK)[:, :count]
    new_coefficients = coefficients
    for step in range(2):
        added = jnp.where(holder == block_ids[step], deltas[step].T.astype(F32), 0.0)
        new_coefficients = new_coefficients + added
        residual = residual - lax.dot_general(
            kern[:, step * BLOCK : (step + 1) * BLOCK],
            deltas[step],
            (((1,), (1,)), ((), ())),
            preferred_element_type=F32,
        )
    return (new_coefficients, residual)


def solution(mesh):
    in_specs = (
        P(("rows", "rrep"), None),
        P(("rows", "rrep")),
        P(("rows", "rrep"), None),
        P("rows", None),
        P("rows", None),
        P(),
    )
    out_specs = (P("rows", None), P(("rows", "rrep"), None))
    return jax.shard_map(shards, mesh=mesh, in_specs=in_specs, out_specs=out_specs, check_vma=False)
```

```python
import functools

import jax
import jax.numpy as jnp
from jax import lax
from jax.experimental import pallas as pl
from jax.experimental.pallas import tpu as pltpu
from jax.sharding import PartitionSpec as P

MESH = pl.DeviceIdType.MESH
HI = lax.Precision.HIGHEST
F32 = jnp.float32
BF16 = jnp.bfloat16
NX, NY, NZ = 4, 4, 8
BLOCK = 512
CLASSES = 1024
VMEM_LIMIT = 52 * 2**20
COPIES = 138
TILE = 128
TILES = BLOCK // TILE
BELOW = [(i, j) for i in range(TILES) for j in range(i)]
EXACT = dict(precision=HI, preferred_element_type=F32)


class Place:
    def __init__(self):
        rows, rrep = lax.axis_index("rows"), lax.axis_index("rrep")
        self.rows, self.rrep = rows, rrep
        self.y, self.z = rows // NZ, rows % NZ
        self.x, self.c = rrep // 2, rrep % 2

    def at_x(self, d):
        other = (self.x + d) % NX
        return other, (self.rows, other * 2 + self.c)

    def at_y(self, d):
        other = (self.y + d) % NY
        return other, (other * NZ + self.z, self.rrep)

    def at_z(self, d):
        other = (self.z + d) % NZ
        return other, (self.y * NZ + other, self.rrep)

    def partner(self):
        return (self.rows, self.x * 2 + 1 - self.c)

    def greet(self, axes):
        barrier = pltpu.get_barrier_semaphore()
        peers = []
        if "x" in axes:
            peers += [self.at_x(d)[1] for d in range(1, NX)]
        if "y" in axes:
            peers += [self.at_y(d)[1] for d in range(1, NY)]
        if "z" in axes:
            peers += [self.at_z(d)[1] for d in range(1, NZ)]
        if "c" in axes:
            peers += [self.partner()]
        for peer in peers:
            pl.semaphore_signal(barrier, inc=1, device_id=peer, device_id_type=MESH)
        return barrier, len(peers)


class Sender:
    def __init__(self, send_sems, recv_sems):
        self.send_sems, self.recv_sems = send_sems, recv_sems
        self.copies = []

    def make(self, src, dst, device):
        i = len(self.copies)
        copy = pltpu.make_async_remote_copy(
            src_ref=src,
            dst_ref=dst,
            send_sem=self.send_sems.at[i],
            recv_sem=self.recv_sems.at[i],
            device_id=device,
            device_id_type=MESH,
        )
        self.copies.append(copy)
        return copy

    def start(self, src, dst, device):
        copy = self.make(src, dst, device)
        copy.start()
        return copy

    def drain(self):
        for copy in self.copies:
            copy.wait_send()


def arrive(copies):
    for copy in copies:
        copy.wait_recv()


def unit_normalize(values):
    wide = values.astype(F32)
    scale = lax.rsqrt(jnp.mean(wide * wide, axis=1, keepdims=True) + 1e-06)
    return (wide * scale).astype(BF16)


def masked_landmarks(me, block_ids, lands, zin):
    share = unit_normalize(lands[...])
    for s in range(2):
        held = jnp.where(block_ids[s] == me.rows, 1.0, 0.0).astype(BF16)
        kept = share * held
        for y in range(NY):
            for g in range(4):
                zin[y, s * 4 + g] = kept[g * 16 : (g + 1) * 16, y * 256 : (y + 1) * 256]


def onehot(labels, shape):
    n = shape[0]
    rows = lax.broadcasted_iota(jnp.int32, (n, n), 0)
    cols = lax.broadcasted_iota(jnp.int32, (n, n), 1)
    spread = jnp.where(rows == cols, jnp.broadcast_to(labels, (n, n)).astype(F32), 0.0)
    column = jnp.sum(spread, axis=1, keepdims=True)
    classes = lax.broadcasted_iota(jnp.int32, shape, 1).astype(F32)
    return jnp.where(classes == column, 1.0, 0.0)


def own_rows(features, labels, scores, xin, rin):
    count = scores.shape[1]
    xin[...] = unit_normalize(features[...])
    target = onehot(labels[...], scores.shape)
    rin[:, CLASSES - 128 :] = jnp.zeros((rin.shape[0], 128), BF16)
    rin[:, :count] = (target - scores[...].astype(F32)).astype(BF16)


def gather_landmarks(me, out, zin, rows, fetches, xin, rin, zall, xp, rp, r1, s1, r2):
    x, y, z, c = me.x, me.y, me.z, me.c
    first = []
    for d in range(1, NY):
        other, device = me.at_y(d)
        first.append(out.start(zin.at[other], r1.at[d - 1], device))
    for fetch in fetches:
        fetch.wait()
    own_rows(*rows, xin, rin)
    swap = [out.start(xin, xp, me.partner()), out.start(rin, rp, me.partner())]
    arrive(first)
    s1[...] = zin[y] + r1[0] + r1[1] + r1[2]
    second = []
    for d in range(1, NZ):
        other, device = me.at_z(d)
        second.append(out.start(s1.at[other], r2.at[d - 1], device))
    arrive(second)
    total = s1[z]
    for d in range(1, NZ):
        total = total + r2[d - 1]
    s, g = z // 4, z % 4
    zall[y, s, x, c, g] = total
    mine = zall.at[y, s, x, c, g]
    arrive([out.start(mine, mine, me.at_z(d)[1]) for d in range(1, NZ)])
    spread_plane(
        me,
        out,
        lambda i, j: zall.at[j, 0, i, c],
        lambda i, j: zall.at[j, 1, i, c],
        lambda i: zall.at[:, 0, i, c],
        lambda j: zall.at[j, 1, :, c],
    )
    arrive(swap)


def spread_plane(me, out, one_a, one_b, column, row):
    x, y = me.x, me.y
    copies = []
    for d in range(1, 4):
        copies.append(out.start(one_a(x, y), one_a(x, y), me.at_y(d)[1]))
        copies.append(out.start(one_b(x, y), one_b(x, y), me.at_x(d)[1]))
    arrive(copies)
    copies = []
    for d in range(1, 4):
        copies.append(out.start(column(x), column(x), me.at_x(d)[1]))
        copies.append(out.start(row(y), row(y), me.at_y(d)[1]))
    across = [
        out.start(column(x), column(x), me.partner()),
        out.start(row(y), row(y), me.partner()),
    ]
    for d in range(1, 4):
        arrive([copies[2 * d - 2]])
        source = (x - d) % NX
        across.append(out.start(column(source), column(source), me.partner()))
        arrive([copies[2 * d - 1]])
        source = (y - d) % NY
        across.append(out.start(row(source), row(source), me.partner()))
    arrive(across)


CONTRACT = (((0,), (0,)), ((), ()))


def columns_of(zall, xref, kern, start):
    rows = xref.shape[0]
    total = None
    for y in range(NY):
        part = lax.dot_general(
            xref[:, y * 256 : (y + 1) * 256],
            zall[y].reshape(2 * BLOCK, 256),
            (((1,), (1,)), ((), ())),
            preferred_element_type=F32,
        )
        total = part if total is None else total + part
    kern[start : start + rows, :] = jnp.exp(total * (1024**-0.5)).astype(BF16)


def eye_mask():
    rows = lax.broadcasted_iota(jnp.int32, (TILE, TILE), 0)
    cols = lax.broadcasted_iota(jnp.int32, (TILE, TILE), 1)
    return rows, cols


def partial_grams(me, kern, gin, diag):
    base = me.c * BLOCK
    rows, cols = eye_mask()
    diagonal = []
    for i in range(TILES):
        left = kern[:, pl.ds(pl.multiple_of(base + i * TILE, TILE), TILE)]
        right = kern[:, pl.ds(pl.multiple_of(base, TILE), (i + 1) * TILE)]
        panel = lax.dot_general(left, right, CONTRACT, preferred_element_type=F32)
        for j in range(i):
            k = BELOW.index((i, j))
            gin[k // NY, k % NY] = panel[:, j * TILE : (j + 1) * TILE].reshape(NZ, 16, TILE)
        diagonal.append(panel[:, i * TILE : (i + 1) * TILE])
    for k in range(2):
        both = jnp.where(rows >= cols, diagonal[2 * k], diagonal[2 * k + 1])
        gin[1, 2 + k] = both.reshape(NZ, 16, TILE)
        lost = jnp.where(rows == cols, diagonal[2 * k + 1], 0.0)
        diag[k : k + 1, :] = jnp.sum(lost, axis=0, keepdims=True)
    diag[2:, :] = jnp.zeros((6, TILE), F32)
    cross = kern[:, pl.ds(pl.multiple_of(BLOCK + me.c * 256, 256), 256)]
    side = lax.dot_general(cross, kern[:, :BLOCK], CONTRACT, preferred_element_type=F32)
    for i in range(2):
        for j in range(TILES):
            block = side[i * TILE : (i + 1) * TILE, j * TILE : (j + 1) * TILE]
            gin[2 + i, j] = block.reshape(NZ, 16, TILE)


def partial_products(me, kern, rin, rp, pin):
    rows = rin.shape[0]
    mine = pl.ds(pl.multiple_of(me.c * BLOCK, BLOCK), BLOCK)

    def step(x, carry):
        part = pl.ds(pl.multiple_of(x * 256, 256), 256)
        own = lax.dot_general(rin[:, part], kern[:rows, mine], CONTRACT, preferred_element_type=F32)
        other = lax.dot_general(rp[:, part], kern[rows:, mine], CONTRACT, preferred_element_type=F32)
        pin[x] = (own + other).reshape(NY, 64, BLOCK)
        return carry

    lax.fori_loop(0, NX, step, 0)


def sum_plane_one(me, out, src, ra, rb, h):
    copies = []
    for d in range(1, 4):
        i, device = me.at_x(d)
        copies.append(out.start(src.at[i, :, 0:h], ra.at[d - 1], device))
        i, device = me.at_y(d)
        copies.append(out.start(src.at[:, i, h : 2 * h], rb.at[d - 1], device))
    return copies


def sum_plane_two(me, out, sa, sb, ra, rb):
    copies = []
    for d in range(1, 4):
        i, device = me.at_y(d)
        copies.append(out.start(sa.at[i], ra.at[d - 1], device))
        i, device = me.at_x(d)
        copies.append(out.start(sb.at[i], rb.at[d - 1], device))
    return copies


def sum_line(me, out, src, received):
    copies = []
    for d in range(1, NZ):
        i, device = me.at_z(d)
        copies.append(out.start(src.at[i], received.at[d - 1], device))
    return copies


def total_of(own, received):
    for d in range(received.shape[0]):
        own = own + received[d]
    return own


def eliminate_rows(values, k, n):
    lane = lax.broadcasted_iota(jnp.int32, (8, n), 1)
    sub = lax.broadcasted_iota(jnp.int32, (8, n), 0)
    rows = values[k : k + 8, :]
    pivots = [jnp.broadcast_to(rows[:, k + q : k + q + 1], (8, n)) for q in range(8)]
    inside = (lane >= k) & (lane < k + 8)
    panel = jnp.where(inside, (lane - k == sub).astype(F32), rows)
    for q in range(8):
        factor = pivots[q]
        inverse = 1.0 / jnp.broadcast_to(factor[q : q + 1, :], (8, n))
        own = sub == q

        def update(block):
            row = jnp.broadcast_to(block[q : q + 1, :], (8, n)) * inverse
            return jnp.where(own, row, block - factor * row)

        for j in range(q + 1, 8):
            pivots[j] = update(pivots[j])
        panel = update(panel)
    return panel


def invert_tile(values, n):
    lane = lax.broadcasted_iota(jnp.int32, (n, n), 1)
    for k in range(0, n, 8):
        panel = eliminate_rows(values, k, n)
        inside = (lane >= k) & (lane < k + 8)
        rest = jnp.where(inside, 0.0, values)
        for q in range(8):
            column = jnp.broadcast_to(values[:, k + q : k + q + 1], (n, n))
            rest = rest - column * jnp.broadcast_to(panel[q : q + 1, :], (n, n))
        parts = ([rest[:k]] if k else []) + [panel] + ([rest[k + 8 :]] if k + 8 < n else [])
        values = jnp.concatenate(parts, axis=0)
    return values


def invert(ref, row, halfway):
    def step(j, carry):
        pl.when(j == TILES // 2)(halfway)
        s = pl.ds(pl.multiple_of(j * TILE, TILE), TILE)
        inverse = invert_tile(ref[s, s], TILE)
        row[...] = jnp.dot(inverse, ref[s, :], **EXACT)
        row[:, s] = inverse
        column = ref[:, s]
        ref[:, s] = jnp.zeros((BLOCK, TILE), F32)
        for i in range(TILES):
            t = slice(i * TILE, (i + 1) * TILE)
            ref[t, :] -= jnp.dot(column[t], row[...], **EXACT)
        ref[s, :] = row[...]
        return carry

    lax.fori_loop(0, TILES, step, 0)


def unpack_grams(ridge, gall, diag, inv, side):
    rows, cols = eye_mask()
    for k, (i, j) in enumerate(BELOW):
        block = gall[k // NY, k % NY].reshape(TILE, TILE)
        inv[i * TILE : (i + 1) * TILE, j * TILE : (j + 1) * TILE] = block
        inv[j * TILE : (j + 1) * TILE, i * TILE : (i + 1) * TILE] = block.T
    for k in range(2):
        both = gall[1, 2 + k].reshape(TILE, TILE)
        turned = both.T
        lower = jnp.where(rows >= cols, both, turned)
        upper = jnp.where(rows < cols, both, turned)
        upper = jnp.where(rows == cols, diag[k : k + 1, :], upper)
        for i, block in ((2 * k, lower), (2 * k + 1, upper)):
            s = slice(i * TILE, (i + 1) * TILE)
            inv[s, s] = block + jnp.where(rows == cols, ridge, 0.0)
    for i in range(2):
        for j in range(TILES):
            side[i * TILE : (i + 1) * TILE, j * TILE : (j + 1) * TILE] = gall[2 + i, j].reshape(TILE, TILE)


def cross_product(delta, side):
    return lax.dot_general(delta.astype(BF16).astype(F32), side, (((1,), (1,)), ((), ())), **EXACT)


def update_kernel(
    ridge,
    block_ids, lands_all, features_all, labels_all, scores_all,
    kout, dout,
    lands, features, labels, scores, fetch_sems, zin, xin, rin, zall, xp, rp, r1, s1, r2,
    kern, gin, diag, pin,
    ga1, gb1, ga, gb, ga2, gb2, g2, g3, gall,
    dx, dxs, dy, dys, dz,
    pa1, pb1, pa, pb, pa2, pb2, p2, p3, prod,
    inv, pivots, side, delta, part, other, opart,
    send_sems, recv_sems,
):
    me = Place()
    greeted = me.greet("xyzc")
    share = lands.shape[0]
    start = pl.multiple_of(me.rrep * share, share)
    fetches = [
        pltpu.make_async_copy(src, dst, fetch_sems.at[i])
        for i, (src, dst) in enumerate(
            (
                (lands_all.at[pl.ds(start, share)], lands),
                (features_all, features),
                (labels_all, labels),
                (scores_all, scores),
            )
        )
    ]
    for fetch in fetches:
        fetch.start()
    fetches[0].wait()
    masked_landmarks(me, block_ids, lands, zin)
    pl.semaphore_wait(*greeted)
    out = Sender(send_sems, recv_sems)
    x, y, z, c = me.x, me.y, me.z, me.c
    rows = xin.shape[0]
    gather_landmarks(me, out, zin, (features, labels, scores), fetches[1:], xin, rin, zall, xp, rp, r1, s1, r2)
    columns_of(zall, xin, kern, 0)
    columns_of(zall, xp, kern, rows)
    partial_grams(me, kern, gin, diag)

    grams = sum_plane_one(me, out, gin, ga1, gb1, 4)
    diags = [out.start(diag, dx.at[d - 1], me.at_x(d)[1]) for d in range(1, NX)]
    kout[...] = kern[:rows, :]
    partial_products(me, kern, rin, rp, pin)
    arrive(grams)
    ga[...] = total_of(gin[x, :, 0:4], ga1)
    gb[...] = total_of(gin[:, y, 4:8], gb1)
    grams = sum_plane_two(me, out, ga, gb, ga2, gb2)
    arrive(diags)
    dxs[...] = total_of(diag[...], dx)
    diags = [out.start(dxs, dy.at[d - 1], me.at_y(d)[1]) for d in range(1, NY)]
    arrive(grams)
    g2[0:4] = total_of(ga[y], ga2)
    g2[4:8] = total_of(gb[x], gb2)
    grams = sum_line(me, out, g2, g3)
    products = sum_plane_one(me, out, pin, pa1, pb1, 32)
    arrive(diags)
    dys[...] = total_of(dxs[...], dy)
    diags = [out.start(dys, dz.at[d - 1], me.at_z(d)[1]) for d in range(1, NZ)]
    arrive(grams)
    gall[x, y, z] = total_of(g2[z], g3)
    mine = gall.at[x, y, z]
    grams = [out.start(mine, mine, me.at_z(d)[1]) for d in range(1, NZ)]
    arrive(grams)
    grams = []
    for d in range(1, 4):
        grams.append(out.start(gall.at[x, y, 0:4], gall.at[x, y, 0:4], me.at_y(d)[1]))
        grams.append(out.start(gall.at[x, y, 4:8], gall.at[x, y, 4:8], me.at_x(d)[1]))
    arrive(products)
    pa[...] = total_of(pin[x, :, 0:32], pa1)
    pb[...] = total_of(pin[:, y, 32:64], pb1)
    arrive(grams)
    grams = []
    for d in range(1, 4):
        grams.append(out.start(gall.at[x, :, 0:4], gall.at[x, :, 0:4], me.at_x(d)[1]))
        grams.append(out.start(gall.at[:, y, 4:8], gall.at[:, y, 4:8], me.at_y(d)[1]))
    products = sum_plane_two(me, out, pa, pb, pa2, pb2)
    arrive(diags)
    lost = total_of(dys[...], dz)
    arrive(grams)

    unpack_grams(ridge, gall, lost, inv, side)
    arrive(products)
    p2[0:4] = total_of(pa[y], pa2).reshape(4, 8, BLOCK)
    p2[4:8] = total_of(pb[x], pb2).reshape(4, 8, BLOCK)
    products = sum_line(me, out, p2, p3)
    returns = [out.make(prod.at[z], prod.at[z], me.at_z(d)[1]) for d in range(1, NZ)]

    def halfway():
        arrive(products)
        prod[z] = total_of(p2[z], p3)
        for copy in returns:
            copy.start()

    invert(inv, pivots, halfway)
    arrive(returns)

    target = prod[...].reshape(64, BLOCK)
    first = jnp.dot(target, inv[...], **EXACT)
    delta[...] = first
    swap = [out.start(delta, other, me.partner())]
    part[...] = cross_product(first, side[...])
    swap.append(out.start(part, opart, me.partner()))
    arrive(swap[:1])
    here = cross_product(other[...], side[...])
    arrive(swap[1:])
    cross = jnp.concatenate([opart[...], here], axis=1)
    second = jnp.dot(target - cross, inv[...], **EXACT)
    dout[c, x, y] = jnp.where(c == 0, first, second).astype(BF16)
    spread_plane(
        me,
        out,
        lambda i, j: dout.at[c, i, j, 0:32],
        lambda i, j: dout.at[c, i, j, 32:64],
        lambda i: dout.at[c, i, :, 0:32],
        lambda j: dout.at[c, :, j, 32:64],
    )
    out.drain()


def update(block_ids, landmarks, features, labels, scores, ridge):
    rows = features.shape[0]
    share = landmarks.shape[0] // 8
    vmem = pl.BlockSpec(memory_space=pltpu.VMEM)
    wide = lambda *shape: pltpu.VMEM(shape, F32)
    half = lambda *shape: pltpu.VMEM(shape, BF16)
    return pl.pallas_call(
        functools.partial(update_kernel, ridge),
        out_shape=(
            jax.ShapeDtypeStruct((rows, 2 * BLOCK), BF16),
            jax.ShapeDtypeStruct((2, NX, NY, 64, BLOCK), BF16),
        ),
        in_specs=[pl.BlockSpec(memory_space=pltpu.SMEM)] + [pl.BlockSpec(memory_space=pltpu.HBM)] * 4,
        out_specs=(vmem,) * 2,
        scratch_shapes=[
            half(share, 1024),
            half(rows, 1024),
            pltpu.VMEM((1, rows), jnp.int32),
            half(rows, scores.shape[1]),
            pltpu.SemaphoreType.DMA((4,)),
            half(NY, NZ, 16, 256),
            half(rows, 1024),
            half(rows, CLASSES),
            half(NY, 2, NX, 2, 4, 16, 256),
            half(rows, 1024),
            half(rows, CLASSES),
            half(NY - 1, NZ, 16, 256),
            half(NZ, 16, 256),
            half(NZ - 1, 16, 256),
            half(2 * rows, 2 * BLOCK),
            wide(NX, NY, NZ, 16, TILE),
            wide(8, TILE),
            wide(NX, NY, 64, BLOCK),
            wide(3, 4, 4, 16, TILE),
            wide(3, 4, 4, 16, TILE),
            wide(4, 4, 16, TILE),
            wide(4, 4, 16, TILE),
            wide(3, 4, 16, TILE),
            wide(3, 4, 16, TILE),
            wide(NZ, 16, TILE),
            wide(NZ - 1, 16, TILE),
            wide(NX, NY, NZ, 16, TILE),
            wide(3, 8, TILE),
            wide(8, TILE),
            wide(3, 8, TILE),
            wide(8, TILE),
            wide(NZ - 1, 8, TILE),
            wide(3, 4, 32, BLOCK),
            wide(3, 4, 32, BLOCK),
            wide(4, 32, BLOCK),
            wide(4, 32, BLOCK),
            wide(3, 32, BLOCK),
            wide(3, 32, BLOCK),
            wide(NZ, 8, BLOCK),
            wide(NZ - 1, 8, BLOCK),
            wide(NZ, 8, BLOCK),
            wide(BLOCK, BLOCK),
            wide(TILE, BLOCK),
            wide(256, BLOCK),
            wide(64, BLOCK),
            wide(64, 256),
            wide(64, BLOCK),
            wide(64, 256),
            pltpu.SemaphoreType.DMA((COPIES,)),
            pltpu.SemaphoreType.DMA((COPIES,)),
        ],
        compiler_params=pltpu.CompilerParams(
            collective_id=0, has_side_effects=True, vmem_limit_bytes=VMEM_LIMIT
        ),
        name="update",
    )(block_ids, landmarks, features, labels, scores)


def finish_kernel(block_ids, kern, deltas, labels, scores, old, new, residual, old_tiles, new_tiles, rest, fetch_sems, store_sems):
    count = scores.shape[1]
    holder = lax.axis_index("rows")
    size = count // 5
    parts = [slice(i * size, (i + 1) * size) for i in range(5)]
    fetches = [
        pltpu.make_async_copy(old.at[parts[i]], old_tiles.at[i], fetch_sems.at[i]) for i in range(5)
    ]
    for fetch in fetches:
        fetch.start()
    total = onehot(labels[...], scores.shape) - scores[...].astype(F32)
    last = (((1,), (1,)), ((), ()))
    for s in range(2):
        moved = lax.dot_general(
            kern[:, s * BLOCK : (s + 1) * BLOCK], deltas[s], last, preferred_element_type=F32
        )
        total = total - moved[:, :count]
    rest[...] = total
    stores = [pltpu.make_async_copy(rest, residual, store_sems.at[5])]
    stores[0].start()
    held = [jnp.where(block_ids[s] == holder, 1.0, 0.0) for s in range(2)]
    for i in range(5):
        added = [deltas[s, parts[i], :].astype(F32) * held[s] for s in range(2)]
        fetches[i].wait()
        new_tiles[i] = old_tiles[i] + (added[0] + added[1])
        stores.append(pltpu.make_async_copy(new_tiles.at[i], new.at[parts[i]], store_sems.at[i]))
        stores[-1].start()
    for store in stores:
        store.wait()


def finish(block_ids, kern, deltas, labels, scores, coefficients):
    vmem = pl.BlockSpec(memory_space=pltpu.VMEM)
    hbm = pl.BlockSpec(memory_space=pltpu.HBM)
    count = scores.shape[1]
    return pl.pallas_call(
        finish_kernel,
        out_shape=(
            jax.ShapeDtypeStruct(coefficients.shape, F32),
            jax.ShapeDtypeStruct(scores.shape, F32),
        ),
        in_specs=[pl.BlockSpec(memory_space=pltpu.SMEM)] + [vmem] * 4 + [hbm],
        out_specs=(hbm,) * 2,
        scratch_shapes=[
            pltpu.VMEM((5, count // 5, BLOCK), F32),
            pltpu.VMEM((5, count // 5, BLOCK), F32),
            pltpu.VMEM(scores.shape, F32),
            pltpu.SemaphoreType.DMA((5,)),
            pltpu.SemaphoreType.DMA((6,)),
        ],
        compiler_params=pltpu.CompilerParams(vmem_limit_bytes=VMEM_LIMIT),
        name="finish",
    )(block_ids, kern, deltas, labels, scores, coefficients)


def shards(features, labels, scores, landmarks, coefficients, block_ids):
    devices_all = lax.axis_size("rows") * lax.axis_size("rrep")
    ridge = float(features.shape[0] * devices_all)
    labels = labels[None, :]
    kern, deltas = update(block_ids, landmarks, features, labels, scores, ridge)
    deltas = deltas.reshape(2, CLASSES, BLOCK)
    new, residual = finish(block_ids, kern, deltas, labels, scores, coefficients.T)
    return new.T, residual


def solution(mesh):
    in_specs = (
        P(("rows", "rrep"), None),
        P(("rows", "rrep")),
        P(("rows", "rrep"), None),
        P("rows", None),
        P("rows", None),
        P(),
    )
    out_specs = (P("rows", None), P(("rows", "rrep"), None))
    return jax.shard_map(shards, mesh=mesh, in_specs=in_specs, out_specs=out_specs, check_vma=False)
```

```python
import functools

import jax
import jax.numpy as jnp
from jax import lax
from jax.experimental import pallas as pl
from jax.experimental.pallas import tpu as pltpu
from jax.sharding import PartitionSpec as P

MESH = pl.DeviceIdType.MESH
HI = lax.Precision.HIGHEST
F32 = jnp.float32
BF16 = jnp.bfloat16
NX, NY, NZ = 4, 4, 8
BLOCK = 512
CLASSES = 1024
VMEM_LIMIT = 62 * 2**20
COPIES = 138
FAR_Z = (4, 3, 5, 2, 6, 1, 7)
FAR = (2, 1, 3)
TILE = 128
TILES = BLOCK // TILE
BELOW = [(i, j) for i in range(TILES) for j in range(i)]
EXACT = dict(precision=HI, preferred_element_type=F32)


class Place:
    def __init__(self):
        rows, rrep = lax.axis_index("rows"), lax.axis_index("rrep")
        self.rows, self.rrep = rows, rrep
        self.y, self.z = rows // NZ, rows % NZ
        self.x, self.c = rrep // 2, rrep % 2

    def at_x(self, d):
        other = (self.x + d) % NX
        return other, (self.rows, other * 2 + self.c)

    def at_y(self, d):
        other = (self.y + d) % NY
        return other, (other * NZ + self.z, self.rrep)

    def at_z(self, d):
        other = (self.z + d) % NZ
        return other, (self.y * NZ + other, self.rrep)

    def partner(self):
        return (self.rows, self.x * 2 + 1 - self.c)

    def greet(self, axes):
        barrier = pltpu.get_barrier_semaphore()
        peers = []
        if "x" in axes:
            peers += [self.at_x(d)[1] for d in FAR]
        if "y" in axes:
            peers += [self.at_y(d)[1] for d in FAR]
        if "z" in axes:
            peers += [self.at_z(d)[1] for d in FAR_Z]
        if "c" in axes:
            peers += [self.partner()]
        for peer in peers:
            pl.semaphore_signal(barrier, inc=1, device_id=peer, device_id_type=MESH)
        return barrier, len(peers)


class Sender:
    def __init__(self, send_sems, recv_sems):
        self.send_sems, self.recv_sems = send_sems, recv_sems
        self.copies = []

    def make(self, src, dst, device):
        i = len(self.copies)
        copy = pltpu.make_async_remote_copy(
            src_ref=src,
            dst_ref=dst,
            send_sem=self.send_sems.at[i],
            recv_sem=self.recv_sems.at[i],
            device_id=device,
            device_id_type=MESH,
        )
        self.copies.append(copy)
        return copy

    def start(self, src, dst, device):
        copy = self.make(src, dst, device)
        copy.start()
        return copy

    def drain(self):
        for copy in self.copies:
            copy.wait_send()


def arrive(copies):
    for copy in copies:
        copy.wait_recv()


def unit_normalize(values):
    wide = values.astype(F32)
    scale = lax.rsqrt(jnp.mean(wide * wide, axis=1, keepdims=True) + 1e-06)
    return (wide * scale).astype(BF16)


def masked_landmarks(me, block_ids, lands, zin):
    share = unit_normalize(lands[...])
    for s in range(2):
        held = jnp.where(block_ids[s] == me.rows, 1.0, 0.0).astype(BF16)
        kept = share * held
        for y in range(NY):
            for g in range(4):
                zin[y, s * 4 + g] = kept[g * 16 : (g + 1) * 16, y * 256 : (y + 1) * 256]


def onehot(labels, shape):
    n = shape[0]
    rows = lax.broadcasted_iota(jnp.int32, (n, n), 0)
    cols = lax.broadcasted_iota(jnp.int32, (n, n), 1)
    spread = jnp.where(rows == cols, jnp.broadcast_to(labels, (n, n)).astype(F32), 0.0)
    column = jnp.sum(spread, axis=1, keepdims=True)
    classes = lax.broadcasted_iota(jnp.int32, shape, 1).astype(F32)
    return jnp.where(classes == column, 1.0, 0.0)


def own_rows(features, labels, scores, xin, rin):
    count = scores.shape[1]
    xin[...] = unit_normalize(features[...])
    target = onehot(labels[...], scores.shape)
    rin[:, CLASSES - 128 :] = jnp.zeros((rin.shape[0], 128), BF16)
    rin[:, :count] = (target - scores[...].astype(F32)).astype(BF16)


def gather_landmarks(me, out, zin, rows, fetches, xin, rin, zall, xp, rp, r1, s1, r2):
    x, y, z, c = me.x, me.y, me.z, me.c
    first = []
    for d in FAR:
        other, device = me.at_y(d)
        first.append(out.start(zin.at[other], r1.at[d - 1], device))
    for fetch in fetches:
        fetch.wait()
    own_rows(*rows, xin, rin)
    swap = [out.start(xin, xp, me.partner()), out.start(rin, rp, me.partner())]
    arrive(first)
    s1[...] = zin[y] + r1[0] + r1[1] + r1[2]
    second = []
    for d in FAR_Z:
        other, device = me.at_z(d)
        second.append(out.start(s1.at[other], r2.at[d - 1], device))
    arrive(second)
    total = s1[z]
    for d in FAR_Z:
        total = total + r2[d - 1]
    s, g = z // 4, z % 4
    zall[y, s, x, c, g] = total
    mine = zall.at[y, s, x, c, g]
    arrive([out.start(mine, mine, me.at_z(d)[1]) for d in FAR_Z])
    spread_plane(
        me,
        out,
        lambda i, j: zall.at[j, 0, i, c],
        lambda i, j: zall.at[j, 1, i, c],
        lambda i: zall.at[:, 0, i, c],
        lambda j: zall.at[j, 1, :, c],
    )
    arrive(swap)


def spread_plane(me, out, one_a, one_b, column, row):
    x, y = me.x, me.y
    copies = []
    for d in FAR:
        copies.append(out.start(one_a(x, y), one_a(x, y), me.at_y(d)[1]))
        copies.append(out.start(one_b(x, y), one_b(x, y), me.at_x(d)[1]))
    arrive(copies)
    columns, rows = {}, {}
    for d in FAR:
        columns[d] = out.start(column(x), column(x), me.at_x(d)[1])
        rows[d] = out.start(row(y), row(y), me.at_y(d)[1])
    across = [
        out.start(column(x), column(x), me.partner()),
        out.start(row(y), row(y), me.partner()),
    ]
    for d in (1, 3, 2):
        arrive([columns[d]])
        source = (x - d) % NX
        across.append(out.start(column(source), column(source), me.partner()))
        arrive([rows[d]])
        source = (y - d) % NY
        across.append(out.start(row(source), row(source), me.partner()))
    arrive(across)


CONTRACT = (((0,), (0,)), ((), ()))


def columns_of(zall, xref, kern, start):
    rows = xref.shape[0]
    total = None
    for y in range(NY):
        part = lax.dot_general(
            xref[:, y * 256 : (y + 1) * 256],
            zall[y].reshape(2 * BLOCK, 256),
            (((1,), (1,)), ((), ())),
            preferred_element_type=F32,
        )
        total = part if total is None else total + part
    kern[start : start + rows, :] = jnp.exp(total * (1024**-0.5)).astype(BF16)


def eye_mask():
    rows = lax.broadcasted_iota(jnp.int32, (TILE, TILE), 0)
    cols = lax.broadcasted_iota(jnp.int32, (TILE, TILE), 1)
    return rows, cols


def partial_grams(me, kern, gin, diag):
    base = me.c * BLOCK
    rows, cols = eye_mask()
    diagonal = []
    for i in range(TILES):
        left = kern[:, pl.ds(pl.multiple_of(base + i * TILE, TILE), TILE)]
        right = kern[:, pl.ds(pl.multiple_of(base, TILE), (i + 1) * TILE)]
        panel = lax.dot_general(left, right, CONTRACT, preferred_element_type=F32)
        for j in range(i):
            k = BELOW.index((i, j))
            gin[k // NY, k % NY] = panel[:, j * TILE : (j + 1) * TILE].reshape(NZ, 16, TILE)
        diagonal.append(panel[:, i * TILE : (i + 1) * TILE])
    for k in range(2):
        both = jnp.where(rows >= cols, diagonal[2 * k], diagonal[2 * k + 1])
        gin[1, 2 + k] = both.reshape(NZ, 16, TILE)
        lost = jnp.where(rows == cols, diagonal[2 * k + 1], 0.0)
        diag[k : k + 1, :] = jnp.sum(lost, axis=0, keepdims=True)
    diag[2:, :] = jnp.zeros((6, TILE), F32)
    cross = kern[:, pl.ds(pl.multiple_of(BLOCK + me.c * 256, 256), 256)]
    side = lax.dot_general(cross, kern[:, :BLOCK], CONTRACT, preferred_element_type=F32)
    for i in range(2):
        for j in range(TILES):
            block = side[i * TILE : (i + 1) * TILE, j * TILE : (j + 1) * TILE]
            gin[2 + i, j] = block.reshape(NZ, 16, TILE)


def partial_products(me, kern, rin, rp, pin):
    rows = rin.shape[0]
    mine = pl.ds(pl.multiple_of(me.c * BLOCK, BLOCK), BLOCK)

    def step(x, carry):
        part = pl.ds(pl.multiple_of(x * 256, 256), 256)
        own = lax.dot_general(rin[:, part], kern[:rows, mine], CONTRACT, preferred_element_type=F32)
        other = lax.dot_general(rp[:, part], kern[rows:, mine], CONTRACT, preferred_element_type=F32)
        pin[x] = (own + other).reshape(NY, 64, BLOCK)
        return carry

    lax.fori_loop(0, NX, step, 0)


def sum_plane_one(me, out, src, ra, rb, h):
    copies = []
    for d in FAR:
        i, device = me.at_x(d)
        copies.append(out.start(src.at[i, :, 0:h], ra.at[d - 1], device))
        i, device = me.at_y(d)
        copies.append(out.start(src.at[:, i, h : 2 * h], rb.at[d - 1], device))
    return copies


def sum_plane_two(me, out, sa, sb, ra, rb):
    copies = []
    for d in FAR:
        i, device = me.at_y(d)
        copies.append(out.start(sa.at[i], ra.at[d - 1], device))
        i, device = me.at_x(d)
        copies.append(out.start(sb.at[i], rb.at[d - 1], device))
    return copies


def sum_line(me, out, src, received):
    copies = []
    for d in FAR_Z:
        i, device = me.at_z(d)
        copies.append(out.start(src.at[i], received.at[d - 1], device))
    return copies


def total_of(own, received):
    for d in range(received.shape[0]):
        own = own + received[d]
    return own


def eliminate_rows(values, k, n):
    lane = lax.broadcasted_iota(jnp.int32, (8, n), 1)
    sub = lax.broadcasted_iota(jnp.int32, (8, n), 0)
    rows = values[k : k + 8, :]
    pivots = [jnp.broadcast_to(rows[:, k + q : k + q + 1], (8, n)) for q in range(8)]
    inside = (lane >= k) & (lane < k + 8)
    panel = jnp.where(inside, (lane - k == sub).astype(F32), rows)
    for q in range(8):
        factor = pivots[q]
        inverse = 1.0 / jnp.broadcast_to(factor[q : q + 1, :], (8, n))
        own = sub == q

        def update(block):
            row = jnp.broadcast_to(block[q : q + 1, :], (8, n)) * inverse
            return jnp.where(own, row, block - factor * row)

        for j in range(q + 1, 8):
            pivots[j] = update(pivots[j])
        panel = update(panel)
    return panel


def invert_tile(values, n):
    lane = lax.broadcasted_iota(jnp.int32, (n, n), 1)
    for k in range(0, n, 8):
        panel = eliminate_rows(values, k, n)
        inside = (lane >= k) & (lane < k + 8)
        rest = jnp.where(inside, 0.0, values)
        for q in range(8):
            column = jnp.broadcast_to(values[:, k + q : k + q + 1], (n, n))
            rest = rest - column * jnp.broadcast_to(panel[q : q + 1, :], (n, n))
        parts = ([rest[:k]] if k else []) + [panel] + ([rest[k + 8 :]] if k + 8 < n else [])
        values = jnp.concatenate(parts, axis=0)
    return values


def invert(ref, row, halfway):
    def step(j, carry):
        pl.when(j == TILES // 2)(halfway)
        s = pl.ds(pl.multiple_of(j * TILE, TILE), TILE)
        inverse = invert_tile(ref[s, s], TILE)
        row[...] = jnp.dot(inverse, ref[s, :], **EXACT)
        row[:, s] = inverse
        column = ref[:, s]
        ref[:, s] = jnp.zeros((BLOCK, TILE), F32)
        for i in range(TILES):
            t = slice(i * TILE, (i + 1) * TILE)
            ref[t, :] -= jnp.dot(column[t], row[...], **EXACT)
        ref[s, :] = row[...]
        return carry

    lax.fori_loop(0, TILES, step, 0)


def unpack_grams(ridge, gall, diag, inv, side):
    rows, cols = eye_mask()
    for k, (i, j) in enumerate(BELOW):
        block = gall[k // NY, k % NY].reshape(TILE, TILE)
        inv[i * TILE : (i + 1) * TILE, j * TILE : (j + 1) * TILE] = block
        inv[j * TILE : (j + 1) * TILE, i * TILE : (i + 1) * TILE] = block.T
    for k in range(2):
        both = gall[1, 2 + k].reshape(TILE, TILE)
        turned = both.T
        lower = jnp.where(rows >= cols, both, turned)
        upper = jnp.where(rows < cols, both, turned)
        upper = jnp.where(rows == cols, diag[k : k + 1, :], upper)
        for i, block in ((2 * k, lower), (2 * k + 1, upper)):
            s = slice(i * TILE, (i + 1) * TILE)
            inv[s, s] = block + jnp.where(rows == cols, ridge, 0.0)
    for i in range(2):
        for j in range(TILES):
            side[i * TILE : (i + 1) * TILE, j * TILE : (j + 1) * TILE] = gall[2 + i, j].reshape(TILE, TILE)


def cross_product(delta, side):
    return lax.dot_general(delta.astype(BF16).astype(F32), side, (((1,), (1,)), ((), ())), **EXACT)


def update_kernel(
    ridge,
    block_ids, lands_all, features_all, labels_all, scores_all,
    kout, dout,
    lands, features, labels, scores, fetch_sems, zin, xin, rin, zall, xp, rp, r1, s1, r2,
    kern, gin, diag, pin,
    ga1, gb1, ga, gb, ga2, gb2, g2, g3, gall,
    dx, dxs, dy, dys, dz,
    pa1, pb1, pa, pb, pa2, pb2, p2, p3, prod,
    inv, pivots, side, delta, part, other, opart,
    send_sems, recv_sems,
):
    me = Place()
    greeted = me.greet("xyzc")
    share = lands.shape[0]
    start = pl.multiple_of(me.rrep * share, share)
    fetches = [
        pltpu.make_async_copy(src, dst, fetch_sems.at[i])
        for i, (src, dst) in enumerate(
            (
                (lands_all.at[pl.ds(start, share)], lands),
                (features_all, features),
                (labels_all, labels),
                (scores_all, scores),
            )
        )
    ]
    for fetch in fetches:
        fetch.start()
    fetches[0].wait()
    masked_landmarks(me, block_ids, lands, zin)
    pl.semaphore_wait(*greeted)
    out = Sender(send_sems, recv_sems)
    x, y, z, c = me.x, me.y, me.z, me.c
    rows = xin.shape[0]
    gather_landmarks(me, out, zin, (features, labels, scores), fetches[1:], xin, rin, zall, xp, rp, r1, s1, r2)
    columns_of(zall, xin, kern, 0)
    columns_of(zall, xp, kern, rows)
    partial_grams(me, kern, gin, diag)

    grams = sum_plane_one(me, out, gin, ga1, gb1, 4)
    diags = [out.start(diag, dx.at[d - 1], me.at_x(d)[1]) for d in FAR]
    kout[...] = kern[:rows, :]
    partial_products(me, kern, rin, rp, pin)
    arrive(grams)
    ga[...] = total_of(gin[x, :, 0:4], ga1)
    gb[...] = total_of(gin[:, y, 4:8], gb1)
    grams = sum_plane_two(me, out, ga, gb, ga2, gb2)
    arrive(diags)
    dxs[...] = total_of(diag[...], dx)
    diags = [out.start(dxs, dy.at[d - 1], me.at_y(d)[1]) for d in FAR]
    arrive(grams)
    g2[0:4] = total_of(ga[y], ga2)
    g2[4:8] = total_of(gb[x], gb2)
    grams = sum_line(me, out, g2, g3)
    products = sum_plane_one(me, out, pin, pa1, pb1, 32)
    arrive(diags)
    dys[...] = total_of(dxs[...], dy)
    diags = [out.start(dys, dz.at[d - 1], me.at_z(d)[1]) for d in FAR_Z]
    arrive(grams)
    gall[x, y, z] = total_of(g2[z], g3)
    mine = gall.at[x, y, z]
    grams = [out.start(mine, mine, me.at_z(d)[1]) for d in FAR_Z]
    arrive(grams)
    grams = []
    for d in FAR:
        grams.append(out.start(gall.at[x, y, 0:4], gall.at[x, y, 0:4], me.at_y(d)[1]))
        grams.append(out.start(gall.at[x, y, 4:8], gall.at[x, y, 4:8], me.at_x(d)[1]))
    arrive(products)
    pa[...] = total_of(pin[x, :, 0:32], pa1)
    pb[...] = total_of(pin[:, y, 32:64], pb1)
    arrive(grams)
    grams = []
    for d in FAR:
        grams.append(out.start(gall.at[x, :, 0:4], gall.at[x, :, 0:4], me.at_x(d)[1]))
        grams.append(out.start(gall.at[:, y, 4:8], gall.at[:, y, 4:8], me.at_y(d)[1]))
    products = sum_plane_two(me, out, pa, pb, pa2, pb2)
    arrive(diags)
    lost = total_of(dys[...], dz)
    arrive(grams)

    unpack_grams(ridge, gall, lost, inv, side)
    arrive(products)
    p2[0:4] = total_of(pa[y], pa2).reshape(4, 8, BLOCK)
    p2[4:8] = total_of(pb[x], pb2).reshape(4, 8, BLOCK)
    products = sum_line(me, out, p2, p3)
    returns = [out.make(prod.at[z], prod.at[z], me.at_z(d)[1]) for d in FAR_Z]

    def halfway():
        arrive(products)
        prod[z] = total_of(p2[z], p3)
        for copy in returns:
            copy.start()

    invert(inv, pivots, halfway)
    arrive(returns)

    target = prod[...].reshape(64, BLOCK)
    first = jnp.dot(target, inv[...], **EXACT)
    delta[...] = first
    swap = [out.start(delta, other, me.partner())]
    part[...] = cross_product(first, side[...])
    swap.append(out.start(part, opart, me.partner()))
    arrive(swap[:1])
    here = cross_product(other[...], side[...])
    arrive(swap[1:])
    cross = jnp.concatenate([opart[...], here], axis=1)
    second = jnp.dot(target - cross, inv[...], **EXACT)
    dout[c, x, y] = jnp.where(c == 0, first, second).astype(BF16)
    spread_plane(
        me,
        out,
        lambda i, j: dout.at[c, i, j, 0:32],
        lambda i, j: dout.at[c, i, j, 32:64],
        lambda i: dout.at[c, i, :, 0:32],
        lambda j: dout.at[c, :, j, 32:64],
    )
    out.drain()


def update(block_ids, landmarks, features, labels, scores, ridge):
    rows = features.shape[0]
    share = landmarks.shape[0] // 8
    vmem = pl.BlockSpec(memory_space=pltpu.VMEM)
    wide = lambda *shape: pltpu.VMEM(shape, F32)
    half = lambda *shape: pltpu.VMEM(shape, BF16)
    return pl.pallas_call(
        functools.partial(update_kernel, ridge),
        out_shape=(
            jax.ShapeDtypeStruct((rows, 2 * BLOCK), BF16),
            jax.ShapeDtypeStruct((2, NX, NY, 64, BLOCK), BF16),
        ),
        in_specs=[pl.BlockSpec(memory_space=pltpu.SMEM)] + [pl.BlockSpec(memory_space=pltpu.HBM)] * 4,
        out_specs=(vmem,) * 2,
        scratch_shapes=[
            half(share, 1024),
            half(rows, 1024),
            pltpu.VMEM((1, rows), jnp.int32),
            half(rows, scores.shape[1]),
            pltpu.SemaphoreType.DMA((4,)),
            half(NY, NZ, 16, 256),
            half(rows, 1024),
            half(rows, CLASSES),
            half(NY, 2, NX, 2, 4, 16, 256),
            half(rows, 1024),
            half(rows, CLASSES),
            half(NY - 1, NZ, 16, 256),
            half(NZ, 16, 256),
            half(NZ - 1, 16, 256),
            half(2 * rows, 2 * BLOCK),
            wide(NX, NY, NZ, 16, TILE),
            wide(8, TILE),
            wide(NX, NY, 64, BLOCK),
            wide(3, 4, 4, 16, TILE),
            wide(3, 4, 4, 16, TILE),
            wide(4, 4, 16, TILE),
            wide(4, 4, 16, TILE),
            wide(3, 4, 16, TILE),
            wide(3, 4, 16, TILE),
            wide(NZ, 16, TILE),
            wide(NZ - 1, 16, TILE),
            wide(NX, NY, NZ, 16, TILE),
            wide(3, 8, TILE),
            wide(8, TILE),
            wide(3, 8, TILE),
            wide(8, TILE),
            wide(NZ - 1, 8, TILE),
            wide(3, 4, 32, BLOCK),
            wide(3, 4, 32, BLOCK),
            wide(4, 32, BLOCK),
            wide(4, 32, BLOCK),
            wide(3, 32, BLOCK),
            wide(3, 32, BLOCK),
            wide(NZ, 8, BLOCK),
            wide(NZ - 1, 8, BLOCK),
            wide(NZ, 8, BLOCK),
            wide(BLOCK, BLOCK),
            wide(TILE, BLOCK),
            wide(256, BLOCK),
            wide(64, BLOCK),
            wide(64, 256),
            wide(64, BLOCK),
            wide(64, 256),
            pltpu.SemaphoreType.DMA((COPIES,)),
            pltpu.SemaphoreType.DMA((COPIES,)),
        ],
        compiler_params=pltpu.CompilerParams(
            collective_id=0, has_side_effects=True, vmem_limit_bytes=VMEM_LIMIT
        ),
        name="update",
    )(block_ids, landmarks, features, labels, scores)


def finish_kernel(block_ids, kern, deltas, labels, scores, old, new, residual, old_tiles, new_tiles, rest, fetch_sems, store_sems):
    count = scores.shape[1]
    holder = lax.axis_index("rows")
    size = count // 5
    parts = [slice(i * size, (i + 1) * size) for i in range(5)]
    fetches = [
        pltpu.make_async_copy(old.at[parts[i]], old_tiles.at[i], fetch_sems.at[i]) for i in range(5)
    ]
    for fetch in fetches:
        fetch.start()
    total = onehot(labels[...], scores.shape) - scores[...].astype(F32)
    last = (((1,), (1,)), ((), ()))
    for s in range(2):
        moved = lax.dot_general(
            kern[:, s * BLOCK : (s + 1) * BLOCK], deltas[s], last, preferred_element_type=F32
        )
        total = total - moved[:, :count]
    rest[...] = total
    stores = [pltpu.make_async_copy(rest, residual, store_sems.at[5])]
    stores[0].start()
    held = [jnp.where(block_ids[s] == holder, 1.0, 0.0) for s in range(2)]
    for i in range(5):
        added = [deltas[s, parts[i], :].astype(F32) * held[s] for s in range(2)]
        fetches[i].wait()
        new_tiles[i] = old_tiles[i] + (added[0] + added[1])
        stores.append(pltpu.make_async_copy(new_tiles.at[i], new.at[parts[i]], store_sems.at[i]))
        stores[-1].start()
    for store in stores:
        store.wait()


def finish(block_ids, kern, deltas, labels, scores, coefficients):
    vmem = pl.BlockSpec(memory_space=pltpu.VMEM)
    hbm = pl.BlockSpec(memory_space=pltpu.HBM)
    count = scores.shape[1]
    return pl.pallas_call(
        finish_kernel,
        out_shape=(
            jax.ShapeDtypeStruct(coefficients.shape, F32),
            jax.ShapeDtypeStruct(scores.shape, F32),
        ),
        in_specs=[pl.BlockSpec(memory_space=pltpu.SMEM)] + [vmem] * 4 + [hbm],
        out_specs=(hbm,) * 2,
        scratch_shapes=[
            pltpu.VMEM((5, count // 5, BLOCK), F32),
            pltpu.VMEM((5, count // 5, BLOCK), F32),
            pltpu.VMEM(scores.shape, F32),
            pltpu.SemaphoreType.DMA((5,)),
            pltpu.SemaphoreType.DMA((6,)),
        ],
        compiler_params=pltpu.CompilerParams(vmem_limit_bytes=VMEM_LIMIT),
        name="finish",
    )(block_ids, kern, deltas, labels, scores, coefficients)


def shards(features, labels, scores, landmarks, coefficients, block_ids):
    devices_all = lax.axis_size("rows") * lax.axis_size("rrep")
    ridge = float(features.shape[0] * devices_all)
    labels = labels[None, :]
    kern, deltas = update(block_ids, landmarks, features, labels, scores, ridge)
    deltas = deltas.reshape(2, CLASSES, BLOCK)
    new, residual = finish(block_ids, kern, deltas, labels, scores, coefficients.T)
    return new.T, residual


def solution(mesh):
    in_specs = (
        P(("rows", "rrep"), None),
        P(("rows", "rrep")),
        P(("rows", "rrep"), None),
        P("rows", None),
        P("rows", None),
        P(),
    )
    out_specs = (P("rows", None), P(("rows", "rrep"), None))
    return jax.shard_map(shards, mesh=mesh, in_specs=in_specs, out_specs=out_specs, check_vma=False)
```

```python
import functools

import jax
import jax.numpy as jnp
from jax import lax
from jax.experimental import pallas as pl
from jax.experimental.pallas import tpu as pltpu
from jax.sharding import PartitionSpec as P

MESH = pl.DeviceIdType.MESH
HI = lax.Precision.HIGHEST
F32 = jnp.float32
BF16 = jnp.bfloat16
NX, NY, NZ = 4, 4, 8
BLOCK = 512
CLASSES = 1024
VMEM_LIMIT = 62 * 2**20
COPIES = 138
FAR_Z = (4, 3, 5, 2, 6, 1, 7)
FAR = (2, 1, 3)
TILE = 128
TILES = BLOCK // TILE
BELOW = [(i, j) for i in range(TILES) for j in range(i)]
EXACT = dict(precision=HI, preferred_element_type=F32)


class Place:
    def __init__(self):
        rows, rrep = lax.axis_index("rows"), lax.axis_index("rrep")
        self.rows, self.rrep = rows, rrep
        self.y, self.z = rows // NZ, rows % NZ
        self.x, self.c = rrep // 2, rrep % 2

    def at_x(self, d):
        other = (self.x + d) % NX
        return other, (self.rows, other * 2 + self.c)

    def at_y(self, d):
        other = (self.y + d) % NY
        return other, (other * NZ + self.z, self.rrep)

    def at_z(self, d):
        other = (self.z + d) % NZ
        return other, (self.y * NZ + other, self.rrep)

    def partner(self):
        return (self.rows, self.x * 2 + 1 - self.c)

    def greet(self, axes):
        barrier = pltpu.get_barrier_semaphore()
        peers = []
        if "x" in axes:
            peers += [self.at_x(d)[1] for d in FAR]
        if "y" in axes:
            peers += [self.at_y(d)[1] for d in FAR]
        if "z" in axes:
            peers += [self.at_z(d)[1] for d in FAR_Z]
        if "c" in axes:
            peers += [self.partner()]
        for peer in peers:
            pl.semaphore_signal(barrier, inc=1, device_id=peer, device_id_type=MESH)
        return barrier, len(peers)


class Sender:
    def __init__(self, send_sems, recv_sems, base=0):
        self.send_sems, self.recv_sems = send_sems, recv_sems
        self.base, self.copies = base, []

    def make(self, src, dst, device):
        i = self.base + len(self.copies)
        copy = pltpu.make_async_remote_copy(
            src_ref=src,
            dst_ref=dst,
            send_sem=self.send_sems.at[i],
            recv_sem=self.recv_sems.at[i],
            device_id=device,
            device_id_type=MESH,
        )
        self.copies.append(copy)
        return copy

    def start(self, src, dst, device):
        copy = self.make(src, dst, device)
        copy.start()
        return copy

    def drain(self):
        for copy in self.copies:
            copy.wait_send()


def arrive(copies):
    for copy in copies:
        copy.wait_recv()


def unit_normalize(values):
    wide = values.astype(F32)
    scale = lax.rsqrt(jnp.mean(wide * wide, axis=1, keepdims=True) + 1e-06)
    return (wide * scale).astype(BF16)


def masked_landmarks(me, block_ids, lands, zin):
    share = unit_normalize(lands[...])
    for s in range(2):
        held = jnp.where(block_ids[s] == me.rows, 1.0, 0.0).astype(BF16)
        kept = share * held
        for y in range(NY):
            for g in range(4):
                zin[y, s * 4 + g] = kept[g * 16 : (g + 1) * 16, y * 256 : (y + 1) * 256]


def onehot(labels, shape):
    n = shape[0]
    rows = lax.broadcasted_iota(jnp.int32, (n, n), 0)
    cols = lax.broadcasted_iota(jnp.int32, (n, n), 1)
    spread = jnp.where(rows == cols, jnp.broadcast_to(labels, (n, n)).astype(F32), 0.0)
    column = jnp.sum(spread, axis=1, keepdims=True)
    classes = lax.broadcasted_iota(jnp.int32, shape, 1).astype(F32)
    return jnp.where(classes == column, 1.0, 0.0)


def own_rows(features, labels, scores, xin, rin):
    count = scores.shape[1]
    xin[...] = unit_normalize(features[...])
    target = onehot(labels[...], scores.shape)
    rin[:, CLASSES - 128 :] = jnp.zeros((rin.shape[0], 128), BF16)
    rin[:, :count] = (target - scores[...].astype(F32)).astype(BF16)


def gather_landmarks(me, out, zin, rows, fetches, xin, rin, zall, xp, rp, r1, s1, r2):
    x, y, z, c = me.x, me.y, me.z, me.c
    first = []
    for d in FAR:
        other, device = me.at_y(d)
        first.append(out.start(zin.at[other], r1.at[d - 1], device))
    for fetch in fetches:
        fetch.wait()
    own_rows(*rows, xin, rin)
    swap = [out.start(xin, xp, me.partner()), out.start(rin, rp, me.partner())]
    arrive(first)
    s1[...] = zin[y] + r1[0] + r1[1] + r1[2]
    second = []
    for d in FAR_Z:
        other, device = me.at_z(d)
        second.append(out.start(s1.at[other], r2.at[d - 1], device))
    arrive(second)
    total = s1[z]
    for d in FAR_Z:
        total = total + r2[d - 1]
    s, g = z // 4, z % 4
    zall[y, s, x, c, g] = total
    mine = zall.at[y, s, x, c, g]
    arrive([out.start(mine, mine, me.at_z(d)[1]) for d in FAR_Z])
    spread_plane(
        me,
        out,
        lambda i, j: zall.at[j, 0, i, c],
        lambda i, j: zall.at[j, 1, i, c],
        lambda i: zall.at[:, 0, i, c],
        lambda j: zall.at[j, 1, :, c],
    )
    arrive(swap)


def spread_plane(me, out, one_a, one_b, column, row):
    x, y = me.x, me.y
    copies = []
    for d in FAR:
        copies.append(out.start(one_a(x, y), one_a(x, y), me.at_y(d)[1]))
        copies.append(out.start(one_b(x, y), one_b(x, y), me.at_x(d)[1]))
    arrive(copies)
    columns, rows = {}, {}
    for d in FAR:
        columns[d] = out.start(column(x), column(x), me.at_x(d)[1])
        rows[d] = out.start(row(y), row(y), me.at_y(d)[1])
    across = [
        out.start(column(x), column(x), me.partner()),
        out.start(row(y), row(y), me.partner()),
    ]
    for d in (1, 3, 2):
        arrive([columns[d]])
        source = (x - d) % NX
        across.append(out.start(column(source), column(source), me.partner()))
        arrive([rows[d]])
        source = (y - d) % NY
        across.append(out.start(row(source), row(source), me.partner()))
    arrive(across)


CONTRACT = (((0,), (0,)), ((), ()))


def columns_of(zall, xref, kern, start):
    rows = xref.shape[0]
    total = None
    for y in range(NY):
        part = lax.dot_general(
            xref[:, y * 256 : (y + 1) * 256],
            zall[y].reshape(2 * BLOCK, 256),
            (((1,), (1,)), ((), ())),
            preferred_element_type=F32,
        )
        total = part if total is None else total + part
    kern[start : start + rows, :] = jnp.exp(total * (1024**-0.5)).astype(BF16)


def eye_mask():
    rows = lax.broadcasted_iota(jnp.int32, (TILE, TILE), 0)
    cols = lax.broadcasted_iota(jnp.int32, (TILE, TILE), 1)
    return rows, cols


def partial_grams(me, kern, gin, diag):
    base = me.c * BLOCK
    rows, cols = eye_mask()
    diagonal = []
    for i in range(TILES):
        left = kern[:, pl.ds(pl.multiple_of(base + i * TILE, TILE), TILE)]
        right = kern[:, pl.ds(pl.multiple_of(base, TILE), (i + 1) * TILE)]
        panel = lax.dot_general(left, right, CONTRACT, preferred_element_type=F32)
        for j in range(i):
            k = BELOW.index((i, j))
            gin[k // NY, k % NY] = panel[:, j * TILE : (j + 1) * TILE].reshape(NZ, 16, TILE)
        diagonal.append(panel[:, i * TILE : (i + 1) * TILE])
    for k in range(2):
        both = jnp.where(rows >= cols, diagonal[2 * k], diagonal[2 * k + 1])
        gin[1, 2 + k] = both.reshape(NZ, 16, TILE)
        lost = jnp.where(rows == cols, diagonal[2 * k + 1], 0.0)
        diag[k : k + 1, :] = jnp.sum(lost, axis=0, keepdims=True)
    diag[2:, :] = jnp.zeros((6, TILE), F32)
    cross = kern[:, pl.ds(pl.multiple_of(BLOCK + me.c * 256, 256), 256)]
    side = lax.dot_general(cross, kern[:, :BLOCK], CONTRACT, preferred_element_type=F32)
    for i in range(2):
        for j in range(TILES):
            block = side[i * TILE : (i + 1) * TILE, j * TILE : (j + 1) * TILE]
            gin[2 + i, j] = block.reshape(NZ, 16, TILE)


def partial_products(me, kern, rin, rp, pin):
    rows = rin.shape[0]
    mine = pl.ds(pl.multiple_of(me.c * BLOCK, BLOCK), BLOCK)

    def step(x, carry):
        part = pl.ds(pl.multiple_of(x * 256, 256), 256)
        own = lax.dot_general(rin[:, part], kern[:rows, mine], CONTRACT, preferred_element_type=F32)
        other = lax.dot_general(rp[:, part], kern[rows:, mine], CONTRACT, preferred_element_type=F32)
        pin[x] = (own + other).reshape(NY, 64, BLOCK)
        return carry

    lax.fori_loop(0, NX, step, 0)


def sum_plane_one(me, out, src, ra, rb, h):
    copies = []
    for d in FAR:
        i, device = me.at_x(d)
        copies.append(out.start(src.at[i, :, 0:h], ra.at[d - 1], device))
        i, device = me.at_y(d)
        copies.append(out.start(src.at[:, i, h : 2 * h], rb.at[d - 1], device))
    return copies


def sum_plane_two(me, out, sa, sb, ra, rb):
    copies = []
    for d in FAR:
        i, device = me.at_y(d)
        copies.append(out.start(sa.at[i], ra.at[d - 1], device))
        i, device = me.at_x(d)
        copies.append(out.start(sb.at[i], rb.at[d - 1], device))
    return copies


def sum_line(me, out, src, received):
    copies = []
    for d in FAR_Z:
        i, device = me.at_z(d)
        copies.append(out.start(src.at[i], received.at[d - 1], device))
    return copies


def total_of(own, received):
    for d in range(received.shape[0]):
        own = own + received[d]
    return own


def eliminate_rows(values, k, n):
    lane = lax.broadcasted_iota(jnp.int32, (8, n), 1)
    sub = lax.broadcasted_iota(jnp.int32, (8, n), 0)
    rows = values[k : k + 8, :]
    pivots = [jnp.broadcast_to(rows[:, k + q : k + q + 1], (8, n)) for q in range(8)]
    inside = (lane >= k) & (lane < k + 8)
    panel = jnp.where(inside, (lane - k == sub).astype(F32), rows)
    for q in range(8):
        factor = pivots[q]
        inverse = 1.0 / jnp.broadcast_to(factor[q : q + 1, :], (8, n))
        own = sub == q

        def update(block):
            row = jnp.broadcast_to(block[q : q + 1, :], (8, n)) * inverse
            return jnp.where(own, row, block - factor * row)

        for j in range(q + 1, 8):
            pivots[j] = update(pivots[j])
        panel = update(panel)
    return panel


def invert_tile(values, n):
    lane = lax.broadcasted_iota(jnp.int32, (n, n), 1)
    for k in range(0, n, 8):
        panel = eliminate_rows(values, k, n)
        inside = (lane >= k) & (lane < k + 8)
        rest = jnp.where(inside, 0.0, values)
        for q in range(8):
            column = jnp.broadcast_to(values[:, k + q : k + q + 1], (n, n))
            rest = rest - column * jnp.broadcast_to(panel[q : q + 1, :], (n, n))
        parts = ([rest[:k]] if k else []) + [panel] + ([rest[k + 8 :]] if k + 8 < n else [])
        values = jnp.concatenate(parts, axis=0)
    return values


def invert(ref, row, halfway):
    def step(j, carry):
        pl.when(j == TILES // 2)(halfway)
        s = pl.ds(pl.multiple_of(j * TILE, TILE), TILE)
        inverse = invert_tile(ref[s, s], TILE)
        row[...] = jnp.dot(inverse, ref[s, :], **EXACT)
        row[:, s] = inverse
        column = ref[:, s]
        ref[:, s] = jnp.zeros((BLOCK, TILE), F32)
        for i in range(TILES):
            t = slice(i * TILE, (i + 1) * TILE)
            ref[t, :] -= jnp.dot(column[t], row[...], **EXACT)
        ref[s, :] = row[...]
        return carry

    lax.fori_loop(0, TILES, step, 0)


def unpack_grams(ridge, gall, diag, inv, side):
    rows, cols = eye_mask()
    for k, (i, j) in enumerate(BELOW):
        block = gall[k // NY, k % NY].reshape(TILE, TILE)
        inv[i * TILE : (i + 1) * TILE, j * TILE : (j + 1) * TILE] = block
        inv[j * TILE : (j + 1) * TILE, i * TILE : (i + 1) * TILE] = block.T
    for k in range(2):
        both = gall[1, 2 + k].reshape(TILE, TILE)
        turned = both.T
        lower = jnp.where(rows >= cols, both, turned)
        upper = jnp.where(rows < cols, both, turned)
        upper = jnp.where(rows == cols, diag[k : k + 1, :], upper)
        for i, block in ((2 * k, lower), (2 * k + 1, upper)):
            s = slice(i * TILE, (i + 1) * TILE)
            inv[s, s] = block + jnp.where(rows == cols, ridge, 0.0)
    for i in range(2):
        for j in range(TILES):
            side[i * TILE : (i + 1) * TILE, j * TILE : (j + 1) * TILE] = gall[2 + i, j].reshape(TILE, TILE)


def cross_product(delta, side):
    return lax.dot_general(delta.astype(BF16).astype(F32), side, (((1,), (1,)), ((), ())), **EXACT)


def update_kernel(
    ridge,
    block_ids, lands_all, features_all, labels_all, scores_all,
    kout, dout,
    lands, features, labels, scores, fetch_sems, zin, xin, rin, zall, xp, rp, r1, s1, r2,
    kern, gin, diag, pin,
    ga1, gb1, ga, gb, ga2, gb2, g2, g3, gall,
    dx, dxs, dy, dys, dz,
    pa1, pb1, pa, pb, pa2, pb2, p2, p3, prod,
    inv, pivots, side, delta, part, other, opart,
    send_sems, recv_sems,
):
    me = Place()
    greeted = me.greet("xyzc")
    share = lands.shape[0]
    start = pl.multiple_of(me.rrep * share, share)
    fetches = [
        pltpu.make_async_copy(src, dst, fetch_sems.at[i])
        for i, (src, dst) in enumerate(
            (
                (lands_all.at[pl.ds(start, share)], lands),
                (features_all, features),
                (labels_all, labels),
                (scores_all, scores),
            )
        )
    ]
    for fetch in fetches:
        fetch.start()
    fetches[0].wait()
    masked_landmarks(me, block_ids, lands, zin)
    pl.semaphore_wait(*greeted)
    out = Sender(send_sems, recv_sems)
    x, y, z, c = me.x, me.y, me.z, me.c
    rows = xin.shape[0]
    gather_landmarks(me, out, zin, (features, labels, scores), fetches[1:], xin, rin, zall, xp, rp, r1, s1, r2)
    columns_of(zall, xin, kern, 0)
    columns_of(zall, xp, kern, rows)
    partial_grams(me, kern, gin, diag)

    grams = sum_plane_one(me, out, gin, ga1, gb1, 4)
    diags = [out.start(diag, dx.at[d - 1], me.at_x(d)[1]) for d in FAR]
    kout[...] = kern[:rows, :]
    partial_products(me, kern, rin, rp, pin)
    arrive(grams)
    ga[...] = total_of(gin[x, :, 0:4], ga1)
    gb[...] = total_of(gin[:, y, 4:8], gb1)
    grams = sum_plane_two(me, out, ga, gb, ga2, gb2)
    arrive(diags)
    dxs[...] = total_of(diag[...], dx)
    diags = [out.start(dxs, dy.at[d - 1], me.at_y(d)[1]) for d in FAR]
    arrive(grams)
    g2[0:4] = total_of(ga[y], ga2)
    g2[4:8] = total_of(gb[x], gb2)
    grams = sum_line(me, out, g2, g3)
    products = sum_plane_one(me, out, pin, pa1, pb1, 32)
    arrive(diags)
    dys[...] = total_of(dxs[...], dy)
    diags = [out.start(dys, dz.at[d - 1], me.at_z(d)[1]) for d in FAR_Z]
    arrive(grams)
    gall[x, y, z] = total_of(g2[z], g3)
    mine = gall.at[x, y, z]
    grams = [out.start(mine, mine, me.at_z(d)[1]) for d in FAR_Z]
    arrive(grams)
    grams = []
    for d in FAR:
        grams.append(out.start(gall.at[x, y, 0:4], gall.at[x, y, 0:4], me.at_y(d)[1]))
        grams.append(out.start(gall.at[x, y, 4:8], gall.at[x, y, 4:8], me.at_x(d)[1]))
    arrive(products)
    pa[...] = total_of(pin[x, :, 0:32], pa1)
    pb[...] = total_of(pin[:, y, 32:64], pb1)
    arrive(grams)
    grams = []
    for d in FAR:
        grams.append(out.start(gall.at[x, :, 0:4], gall.at[x, :, 0:4], me.at_x(d)[1]))
        grams.append(out.start(gall.at[:, y, 4:8], gall.at[:, y, 4:8], me.at_y(d)[1]))
    products = sum_plane_two(me, out, pa, pb, pa2, pb2)
    arrive(diags)
    lost = total_of(dys[...], dz)
    arrive(grams)

    unpack_grams(ridge, gall, lost, inv, side)
    arrive(products)
    p2[0:4] = total_of(pa[y], pa2).reshape(4, 8, BLOCK)
    p2[4:8] = total_of(pb[x], pb2).reshape(4, 8, BLOCK)
    products = sum_line(me, out, p2, p3)
    returns = [out.make(prod.at[z], prod.at[z], me.at_z(d)[1]) for d in FAR_Z]

    def halfway():
        arrive(products)
        prod[z] = total_of(p2[z], p3)
        for copy in returns:
            copy.start()

    invert(inv, pivots, halfway)
    arrive(returns)

    used = len(out.copies)
    gifts = Sender(send_sems, recv_sems, used)
    gifts.make(delta, other, me.partner())
    gifts.make(part, opart, me.partner())

    def share(value):
        last = Sender(send_sems, recv_sems, used + 2)
        dout[c, x, y] = value.astype(BF16)
        spread_plane(
            me,
            last,
            lambda i, j: dout.at[c, i, j, 0:32],
            lambda i, j: dout.at[c, i, j, 32:64],
            lambda i: dout.at[c, i, :, 0:32],
            lambda j: dout.at[c, :, j, 32:64],
        )
        last.drain()

    @pl.when(c == 0)
    def _():
        first = jnp.dot(prod[...].reshape(64, BLOCK), inv[...], **EXACT)
        delta[...] = first
        gifts.copies[0].start()
        part[...] = cross_product(first, side[...])
        gifts.copies[1].start()
        share(first)
        gifts.drain()

    @pl.when(c == 1)
    def _():
        arrive(gifts.copies[:1])
        here = cross_product(other[...], side[...])
        arrive(gifts.copies[1:])
        cross = jnp.concatenate([opart[...], here], axis=1)
        share(jnp.dot(prod[...].reshape(64, BLOCK) - cross, inv[...], **EXACT))

    out.drain()


def update(block_ids, landmarks, features, labels, scores, ridge):
    rows = features.shape[0]
    share = landmarks.shape[0] // 8
    vmem = pl.BlockSpec(memory_space=pltpu.VMEM)
    wide = lambda *shape: pltpu.VMEM(shape, F32)
    half = lambda *shape: pltpu.VMEM(shape, BF16)
    return pl.pallas_call(
        functools.partial(update_kernel, ridge),
        out_shape=(
            jax.ShapeDtypeStruct((rows, 2 * BLOCK), BF16),
            jax.ShapeDtypeStruct((2, NX, NY, 64, BLOCK), BF16),
        ),
        in_specs=[pl.BlockSpec(memory_space=pltpu.SMEM)] + [pl.BlockSpec(memory_space=pltpu.HBM)] * 4,
        out_specs=(vmem,) * 2,
        scratch_shapes=[
            half(share, 1024),
            half(rows, 1024),
            pltpu.VMEM((1, rows), jnp.int32),
            half(rows, scores.shape[1]),
            pltpu.SemaphoreType.DMA((4,)),
            half(NY, NZ, 16, 256),
            half(rows, 1024),
            half(rows, CLASSES),
            half(NY, 2, NX, 2, 4, 16, 256),
            half(rows, 1024),
            half(rows, CLASSES),
            half(NY - 1, NZ, 16, 256),
            half(NZ, 16, 256),
            half(NZ - 1, 16, 256),
            half(2 * rows, 2 * BLOCK),
            wide(NX, NY, NZ, 16, TILE),
            wide(8, TILE),
            wide(NX, NY, 64, BLOCK),
            wide(3, 4, 4, 16, TILE),
            wide(3, 4, 4, 16, TILE),
            wide(4, 4, 16, TILE),
            wide(4, 4, 16, TILE),
            wide(3, 4, 16, TILE),
            wide(3, 4, 16, TILE),
            wide(NZ, 16, TILE),
            wide(NZ - 1, 16, TILE),
            wide(NX, NY, NZ, 16, TILE),
            wide(3, 8, TILE),
            wide(8, TILE),
            wide(3, 8, TILE),
            wide(8, TILE),
            wide(NZ - 1, 8, TILE),
            wide(3, 4, 32, BLOCK),
            wide(3, 4, 32, BLOCK),
            wide(4, 32, BLOCK),
            wide(4, 32, BLOCK),
            wide(3, 32, BLOCK),
            wide(3, 32, BLOCK),
            wide(NZ, 8, BLOCK),
            wide(NZ - 1, 8, BLOCK),
            wide(NZ, 8, BLOCK),
            wide(BLOCK, BLOCK),
            wide(TILE, BLOCK),
            wide(256, BLOCK),
            wide(64, BLOCK),
            wide(64, 256),
            wide(64, BLOCK),
            wide(64, 256),
            pltpu.SemaphoreType.DMA((COPIES,)),
            pltpu.SemaphoreType.DMA((COPIES,)),
        ],
        compiler_params=pltpu.CompilerParams(
            collective_id=0, has_side_effects=True, vmem_limit_bytes=VMEM_LIMIT
        ),
        name="update",
    )(block_ids, landmarks, features, labels, scores)


def finish_kernel(block_ids, kern, deltas, labels, scores, old, new, residual, old_tiles, new_tiles, rest, fetch_sems, store_sems):
    count = scores.shape[1]
    holder = lax.axis_index("rows")
    size = count // 5
    parts = [slice(i * size, (i + 1) * size) for i in range(5)]
    fetches = [
        pltpu.make_async_copy(old.at[parts[i]], old_tiles.at[i], fetch_sems.at[i]) for i in range(5)
    ]
    for fetch in fetches:
        fetch.start()
    total = onehot(labels[...], scores.shape) - scores[...].astype(F32)
    last = (((1,), (1,)), ((), ()))
    for s in range(2):
        moved = lax.dot_general(
            kern[:, s * BLOCK : (s + 1) * BLOCK], deltas[s], last, preferred_element_type=F32
        )
        total = total - moved[:, :count]
    rest[...] = total
    stores = [pltpu.make_async_copy(rest, residual, store_sems.at[5])]
    stores[0].start()
    held = [jnp.where(block_ids[s] == holder, 1.0, 0.0) for s in range(2)]
    for i in range(5):
        added = [deltas[s, parts[i], :].astype(F32) * held[s] for s in range(2)]
        fetches[i].wait()
        new_tiles[i] = old_tiles[i] + (added[0] + added[1])
        stores.append(pltpu.make_async_copy(new_tiles.at[i], new.at[parts[i]], store_sems.at[i]))
        stores[-1].start()
    for store in stores:
        store.wait()


def finish(block_ids, kern, deltas, labels, scores, coefficients):
    vmem = pl.BlockSpec(memory_space=pltpu.VMEM)
    hbm = pl.BlockSpec(memory_space=pltpu.HBM)
    count = scores.shape[1]
    return pl.pallas_call(
        finish_kernel,
        out_shape=(
            jax.ShapeDtypeStruct(coefficients.shape, F32),
            jax.ShapeDtypeStruct(scores.shape, F32),
        ),
        in_specs=[pl.BlockSpec(memory_space=pltpu.SMEM)] + [vmem] * 4 + [hbm],
        out_specs=(hbm,) * 2,
        scratch_shapes=[
            pltpu.VMEM((5, count // 5, BLOCK), F32),
            pltpu.VMEM((5, count // 5, BLOCK), F32),
            pltpu.VMEM(scores.shape, F32),
            pltpu.SemaphoreType.DMA((5,)),
            pltpu.SemaphoreType.DMA((6,)),
        ],
        compiler_params=pltpu.CompilerParams(vmem_limit_bytes=VMEM_LIMIT),
        name="finish",
    )(block_ids, kern, deltas, labels, scores, coefficients)


def shards(features, labels, scores, landmarks, coefficients, block_ids):
    devices_all = lax.axis_size("rows") * lax.axis_size("rrep")
    ridge = float(features.shape[0] * devices_all)
    labels = labels[None, :]
    kern, deltas = update(block_ids, landmarks, features, labels, scores, ridge)
    deltas = deltas.reshape(2, CLASSES, BLOCK)
    new, residual = finish(block_ids, kern, deltas, labels, scores, coefficients.T)
    return new.T, residual


def solution(mesh):
    in_specs = (
        P(("rows", "rrep"), None),
        P(("rows", "rrep")),
        P(("rows", "rrep"), None),
        P("rows", None),
        P("rows", None),
        P(),
    )
    out_specs = (P("rows", None), P(("rows", "rrep"), None))
    return jax.shard_map(shards, mesh=mesh, in_specs=in_specs, out_specs=out_specs, check_vma=False)
```

```python
import functools

import jax
import jax.numpy as jnp
from jax import lax
from jax.experimental import pallas as pl
from jax.experimental.pallas import tpu as pltpu
from jax.sharding import PartitionSpec as P

MESH = pl.DeviceIdType.MESH
HI = lax.Precision.HIGHEST
F32 = jnp.float32
BF16 = jnp.bfloat16
NX, NY, NZ = 4, 4, 8
BLOCK = 512
CLASSES = 1024
VMEM_LIMIT = 62 * 2**20
COPIES = 138
FAR_Z = (4, 3, 5, 2, 6, 1, 7)
FAR = (2, 1, 3)
TILE = 128
TILES = BLOCK // TILE
BELOW = [(i, j) for i in range(TILES) for j in range(i)]
EXACT = dict(precision=HI, preferred_element_type=F32)


class Place:
    def __init__(self):
        rows, rrep = lax.axis_index("rows"), lax.axis_index("rrep")
        self.rows, self.rrep = rows, rrep
        self.y, self.z = rows // NZ, rows % NZ
        self.x, self.c = rrep // 2, rrep % 2

    def at_x(self, d):
        other = (self.x + d) % NX
        return other, (self.rows, other * 2 + self.c)

    def at_y(self, d):
        other = (self.y + d) % NY
        return other, (other * NZ + self.z, self.rrep)

    def at_z(self, d):
        other = (self.z + d) % NZ
        return other, (self.y * NZ + other, self.rrep)

    def partner(self):
        return (self.rows, self.x * 2 + 1 - self.c)

    def greet(self, axes):
        barrier = pltpu.get_barrier_semaphore()
        peers = []
        if "x" in axes:
            peers += [self.at_x(d)[1] for d in FAR]
        if "y" in axes:
            peers += [self.at_y(d)[1] for d in FAR]
        if "z" in axes:
            peers += [self.at_z(d)[1] for d in FAR_Z]
        if "c" in axes:
            peers += [self.partner()]
        for peer in peers:
            pl.semaphore_signal(barrier, inc=1, device_id=peer, device_id_type=MESH)
        return barrier, len(peers)


class Sender:
    def __init__(self, send_sems, recv_sems, base=0):
        self.send_sems, self.recv_sems = send_sems, recv_sems
        self.base, self.copies = base, []

    def make(self, src, dst, device):
        i = self.base + len(self.copies)
        copy = pltpu.make_async_remote_copy(
            src_ref=src,
            dst_ref=dst,
            send_sem=self.send_sems.at[i],
            recv_sem=self.recv_sems.at[i],
            device_id=device,
            device_id_type=MESH,
        )
        self.copies.append(copy)
        return copy

    def start(self, src, dst, device):
        copy = self.make(src, dst, device)
        copy.start()
        return copy

    def drain(self):
        for copy in self.copies:
            copy.wait_send()


def arrive(copies):
    for copy in copies:
        copy.wait_recv()


def unit_normalize(values):
    wide = values.astype(F32)
    scale = lax.rsqrt(jnp.mean(wide * wide, axis=1, keepdims=True) + 1e-06)
    return (wide * scale).astype(BF16)


def masked_landmarks(me, block_ids, lands, zin):
    share = unit_normalize(lands[...])
    for s in range(2):
        held = jnp.where(block_ids[s] == me.rows, 1.0, 0.0).astype(BF16)
        kept = share * held
        for y in range(NY):
            for g in range(4):
                zin[y, s * 4 + g] = kept[g * 16 : (g + 1) * 16, y * 256 : (y + 1) * 256]


def onehot(labels, shape):
    n = shape[0]
    rows = lax.broadcasted_iota(jnp.int32, (n, n), 0)
    cols = lax.broadcasted_iota(jnp.int32, (n, n), 1)
    spread = jnp.where(rows == cols, jnp.broadcast_to(labels, (n, n)).astype(F32), 0.0)
    column = jnp.sum(spread, axis=1, keepdims=True)
    classes = lax.broadcasted_iota(jnp.int32, shape, 1).astype(F32)
    return jnp.where(classes == column, 1.0, 0.0)


def own_rows(features, labels, scores, xin, rin):
    count = scores.shape[1]
    xin[...] = unit_normalize(features[...])
    target = onehot(labels[...], scores.shape)
    rin[:, CLASSES - 128 :] = jnp.zeros((rin.shape[0], 128), BF16)
    rin[:, :count] = (target - scores[...].astype(F32)).astype(BF16)


def gather_landmarks(me, out, zin, rows, fetches, xin, rin, zall, xp, rp, r1, s1, r2):
    x, y, z, c = me.x, me.y, me.z, me.c
    first = []
    for d in FAR:
        other, device = me.at_y(d)
        first.append(out.start(zin.at[other], r1.at[d - 1], device))
    for fetch in fetches:
        fetch.wait()
    own_rows(*rows, xin, rin)
    swap = [out.start(xin, xp, me.partner()), out.start(rin, rp, me.partner())]
    arrive(first)
    s1[...] = zin[y] + r1[0] + r1[1] + r1[2]
    second = []
    for d in FAR_Z:
        other, device = me.at_z(d)
        second.append(out.start(s1.at[other], r2.at[d - 1], device))
    arrive(second)
    total = s1[z]
    for d in FAR_Z:
        total = total + r2[d - 1]
    s, g = z // 4, z % 4
    zall[y, s, x, c, g] = total
    mine = zall.at[y, s, x, c, g]
    arrive([out.start(mine, mine, me.at_z(d)[1]) for d in FAR_Z])
    spread_plane(
        me,
        out,
        lambda i, j: zall.at[j, 0, i, c],
        lambda i, j: zall.at[j, 1, i, c],
        lambda i: zall.at[:, 0, i, c],
        lambda j: zall.at[j, 1, :, c],
    )
    arrive(swap)


def spread_plane(me, out, one_a, one_b, column, row):
    x, y = me.x, me.y
    copies = []
    for d in FAR:
        copies.append(out.start(one_a(x, y), one_a(x, y), me.at_y(d)[1]))
        copies.append(out.start(one_b(x, y), one_b(x, y), me.at_x(d)[1]))
    arrive(copies)
    columns, rows = {}, {}
    for d in FAR:
        columns[d] = out.start(column(x), column(x), me.at_x(d)[1])
        rows[d] = out.start(row(y), row(y), me.at_y(d)[1])
    across = [
        out.start(column(x), column(x), me.partner()),
        out.start(row(y), row(y), me.partner()),
    ]
    for d in (1, 3, 2):
        arrive([columns[d]])
        source = (x - d) % NX
        across.append(out.start(column(source), column(source), me.partner()))
        arrive([rows[d]])
        source = (y - d) % NY
        across.append(out.start(row(source), row(source), me.partner()))
    arrive(across)


CONTRACT = (((0,), (0,)), ((), ()))


def columns_of(zall, xref, kern, start):
    rows = xref.shape[0]
    total = None
    for y in range(NY):
        part = lax.dot_general(
            xref[:, y * 256 : (y + 1) * 256],
            zall[y].reshape(2 * BLOCK, 256),
            (((1,), (1,)), ((), ())),
            preferred_element_type=F32,
        )
        total = part if total is None else total + part
    kern[start : start + rows, :] = jnp.exp(total * (1024**-0.5)).astype(BF16)


def eye_mask():
    rows = lax.broadcasted_iota(jnp.int32, (TILE, TILE), 0)
    cols = lax.broadcasted_iota(jnp.int32, (TILE, TILE), 1)
    return rows, cols


def partial_grams(me, kern, gin, diag):
    base = me.c * BLOCK
    rows, cols = eye_mask()
    diagonal = []
    for i in range(TILES):
        left = kern[:, pl.ds(pl.multiple_of(base + i * TILE, TILE), TILE)]
        right = kern[:, pl.ds(pl.multiple_of(base, TILE), (i + 1) * TILE)]
        panel = lax.dot_general(left, right, CONTRACT, preferred_element_type=F32)
        for j in range(i):
            k = BELOW.index((i, j))
            gin[k // NY, k % NY] = panel[:, j * TILE : (j + 1) * TILE].reshape(NZ, 16, TILE)
        diagonal.append(panel[:, i * TILE : (i + 1) * TILE])
    for k in range(2):
        both = jnp.where(rows >= cols, diagonal[2 * k], diagonal[2 * k + 1])
        gin[1, 2 + k] = both.reshape(NZ, 16, TILE)
        lost = jnp.where(rows == cols, diagonal[2 * k + 1], 0.0)
        diag[k : k + 1, :] = jnp.sum(lost, axis=0, keepdims=True)
    diag[2:, :] = jnp.zeros((6, TILE), F32)
    cross = kern[:, pl.ds(pl.multiple_of(BLOCK + me.c * 256, 256), 256)]
    side = lax.dot_general(cross, kern[:, :BLOCK], CONTRACT, preferred_element_type=F32)
    for i in range(2):
        for j in range(TILES):
            block = side[i * TILE : (i + 1) * TILE, j * TILE : (j + 1) * TILE]
            gin[2 + i, j] = block.reshape(NZ, 16, TILE)


def partial_products(me, kern, rin, rp, pin):
    rows = rin.shape[0]
    mine = pl.ds(pl.multiple_of(me.c * BLOCK, BLOCK), BLOCK)

    def step(x, carry):
        part = pl.ds(pl.multiple_of(x * 256, 256), 256)
        own = lax.dot_general(rin[:, part], kern[:rows, mine], CONTRACT, preferred_element_type=F32)
        other = lax.dot_general(rp[:, part], kern[rows:, mine], CONTRACT, preferred_element_type=F32)
        pin[x] = (own + other).reshape(NY, 64, BLOCK)
        return carry

    lax.fori_loop(0, NX, step, 0)


def sum_plane_one(me, out, src, ra, rb, h):
    copies = []
    for d in FAR:
        i, device = me.at_x(d)
        copies.append(out.start(src.at[i, :, 0:h], ra.at[d - 1], device))
        i, device = me.at_y(d)
        copies.append(out.start(src.at[:, i, h : 2 * h], rb.at[d - 1], device))
    return copies


def sum_plane_two(me, out, sa, sb, ra, rb):
    copies = []
    for d in FAR:
        i, device = me.at_y(d)
        copies.append(out.start(sa.at[i], ra.at[d - 1], device))
        i, device = me.at_x(d)
        copies.append(out.start(sb.at[i], rb.at[d - 1], device))
    return copies


def sum_line(me, out, src, received):
    copies = []
    for d in FAR_Z:
        i, device = me.at_z(d)
        copies.append(out.start(src.at[i], received.at[d - 1], device))
    return copies


def total_of(own, received):
    for d in range(received.shape[0]):
        own = own + received[d]
    return own


def eliminate_rows(values, k, n):
    lane = lax.broadcasted_iota(jnp.int32, (8, n), 1)
    sub = lax.broadcasted_iota(jnp.int32, (8, n), 0)
    rows = values[k : k + 8, :]
    pivots = [jnp.broadcast_to(rows[:, k + q : k + q + 1], (8, n)) for q in range(8)]
    inside = (lane >= k) & (lane < k + 8)
    panel = jnp.where(inside, (lane - k == sub).astype(F32), rows)
    for q in range(8):
        factor = pivots[q]
        inverse = 1.0 / jnp.broadcast_to(factor[q : q + 1, :], (8, n))
        own = sub == q

        def update(block):
            row = jnp.broadcast_to(block[q : q + 1, :], (8, n)) * inverse
            return jnp.where(own, row, block - factor * row)

        for j in range(q + 1, 8):
            pivots[j] = update(pivots[j])
        panel = update(panel)
    return panel


def invert_tile(values, n):
    lane = lax.broadcasted_iota(jnp.int32, (n, n), 1)
    for k in range(0, n, 8):
        panel = eliminate_rows(values, k, n)
        inside = (lane >= k) & (lane < k + 8)
        rest = jnp.where(inside, 0.0, values)
        for q in range(8):
            column = jnp.broadcast_to(values[:, k + q : k + q + 1], (n, n))
            rest = rest - column * jnp.broadcast_to(panel[q : q + 1, :], (n, n))
        parts = ([rest[:k]] if k else []) + [panel] + ([rest[k + 8 :]] if k + 8 < n else [])
        values = jnp.concatenate(parts, axis=0)
    return values


def invert(ref, row, halfway):
    def step(j, carry):
        pl.when(j == TILES // 2)(halfway)
        s = pl.ds(pl.multiple_of(j * TILE, TILE), TILE)
        inverse = invert_tile(ref[s, s], TILE)
        row[...] = jnp.dot(inverse, ref[s, :], **EXACT)
        row[:, s] = inverse
        column = ref[:, s]
        ref[:, s] = jnp.zeros((BLOCK, TILE), F32)
        for i in range(TILES):
            t = slice(i * TILE, (i + 1) * TILE)
            ref[t, :] -= jnp.dot(column[t], row[...], **EXACT)
        ref[s, :] = row[...]
        return carry

    lax.fori_loop(0, TILES, step, 0)


def unpack_grams(ridge, gall, diag, inv, side):
    rows, cols = eye_mask()
    for k, (i, j) in enumerate(BELOW):
        block = gall[k // NY, k % NY].reshape(TILE, TILE)
        inv[i * TILE : (i + 1) * TILE, j * TILE : (j + 1) * TILE] = block
        inv[j * TILE : (j + 1) * TILE, i * TILE : (i + 1) * TILE] = block.T
    for k in range(2):
        both = gall[1, 2 + k].reshape(TILE, TILE)
        turned = both.T
        lower = jnp.where(rows >= cols, both, turned)
        upper = jnp.where(rows < cols, both, turned)
        upper = jnp.where(rows == cols, diag[k : k + 1, :], upper)
        for i, block in ((2 * k, lower), (2 * k + 1, upper)):
            s = slice(i * TILE, (i + 1) * TILE)
            inv[s, s] = block + jnp.where(rows == cols, ridge, 0.0)
    for i in range(2):
        for j in range(TILES):
            side[i * TILE : (i + 1) * TILE, j * TILE : (j + 1) * TILE] = gall[2 + i, j].reshape(TILE, TILE)


def cross_product(delta, side):
    return lax.dot_general(delta.astype(BF16).astype(F32), side, (((1,), (1,)), ((), ())), **EXACT)


def update_kernel(
    ridge,
    block_ids, lands_all, features_all, labels_all, scores_all,
    kout, dout,
    lands, features, labels, scores, fetch_sems, zin, xin, rin, zall, xp, rp, r1, s1, r2,
    kern, gin, diag, pin,
    ga1, gb1, ga, gb, ga2, gb2, g2, g3, gall,
    dx, dxs, dy, dys, dz,
    pa1, pb1, pa, pb, pa2, pb2, p2, p3, prod,
    inv, pivots, side, delta, part, other, opart,
    send_sems, recv_sems,
):
    me = Place()
    greeted = me.greet("xyzc")
    share = lands.shape[0]
    start = pl.multiple_of(me.rrep * share, share)
    fetches = [
        pltpu.make_async_copy(src, dst, fetch_sems.at[i])
        for i, (src, dst) in enumerate(
            (
                (lands_all.at[pl.ds(start, share)], lands),
                (features_all, features),
                (labels_all, labels),
                (scores_all, scores),
            )
        )
    ]
    for fetch in fetches:
        fetch.start()
    fetches[0].wait()
    masked_landmarks(me, block_ids, lands, zin)
    pl.semaphore_wait(*greeted)
    out = Sender(send_sems, recv_sems)
    x, y, z, c = me.x, me.y, me.z, me.c
    rows = xin.shape[0]
    gather_landmarks(me, out, zin, (features, labels, scores), fetches[1:], xin, rin, zall, xp, rp, r1, s1, r2)
    columns_of(zall, xin, kern, 0)
    columns_of(zall, xp, kern, rows)
    partial_grams(me, kern, gin, diag)

    grams = sum_plane_one(me, out, gin, ga1, gb1, 4)
    diags = [out.start(diag, dx.at[d - 1], me.at_x(d)[1]) for d in FAR]
    kout[...] = kern[:rows, :]
    partial_products(me, kern, rin, rp, pin)
    arrive(grams)
    ga[...] = total_of(gin[x, :, 0:4], ga1)
    gb[...] = total_of(gin[:, y, 4:8], gb1)
    grams = sum_plane_two(me, out, ga, gb, ga2, gb2)
    arrive(diags)
    dxs[...] = total_of(diag[...], dx)
    diags = [out.start(dxs, dy.at[d - 1], me.at_y(d)[1]) for d in FAR]
    arrive(grams)
    g2[0:4] = total_of(ga[y], ga2)
    g2[4:8] = total_of(gb[x], gb2)
    grams = sum_line(me, out, g2, g3)
    products = sum_plane_one(me, out, pin, pa1, pb1, 32)
    arrive(diags)
    dys[...] = total_of(dxs[...], dy)
    diags = [out.start(dys, dz.at[d - 1], me.at_z(d)[1]) for d in FAR_Z]
    arrive(grams)
    gall[x, y, z] = total_of(g2[z], g3)
    mine = gall.at[x, y, z]
    grams = [out.start(mine, mine, me.at_z(d)[1]) for d in FAR_Z]
    arrive(grams)
    grams = []
    for d in FAR:
        grams.append(out.start(gall.at[x, y, 0:4], gall.at[x, y, 0:4], me.at_y(d)[1]))
        grams.append(out.start(gall.at[x, y, 4:8], gall.at[x, y, 4:8], me.at_x(d)[1]))
    arrive(products)
    pa[...] = total_of(pin[x, :, 0:32], pa1)
    pb[...] = total_of(pin[:, y, 32:64], pb1)
    products = sum_plane_two(me, out, pa, pb, pa2, pb2)
    arrive(grams)
    grams = []
    for d in FAR:
        grams.append(out.start(gall.at[x, :, 0:4], gall.at[x, :, 0:4], me.at_x(d)[1]))
        grams.append(out.start(gall.at[:, y, 4:8], gall.at[:, y, 4:8], me.at_y(d)[1]))
    arrive(diags)
    lost = total_of(dys[...], dz)
    arrive(grams)

    unpack_grams(ridge, gall, lost, inv, side)
    arrive(products)
    p2[0:4] = total_of(pa[y], pa2).reshape(4, 8, BLOCK)
    p2[4:8] = total_of(pb[x], pb2).reshape(4, 8, BLOCK)
    products = sum_line(me, out, p2, p3)
    returns = [out.make(prod.at[z], prod.at[z], me.at_z(d)[1]) for d in FAR_Z]

    def halfway():
        arrive(products)
        prod[z] = total_of(p2[z], p3)
        for copy in returns:
            copy.start()

    invert(inv, pivots, halfway)
    arrive(returns)

    used = len(out.copies)
    gifts = Sender(send_sems, recv_sems, used)
    gifts.make(delta, other, me.partner())
    gifts.make(part, opart, me.partner())

    def share(value):
        last = Sender(send_sems, recv_sems, used + 2)
        dout[c, x, y] = value.astype(BF16)
        spread_plane(
            me,
            last,
            lambda i, j: dout.at[c, i, j, 0:32],
            lambda i, j: dout.at[c, i, j, 32:64],
            lambda i: dout.at[c, i, :, 0:32],
            lambda j: dout.at[c, :, j, 32:64],
        )
        last.drain()

    @pl.when(c == 0)
    def _():
        first = jnp.dot(prod[...].reshape(64, BLOCK), inv[...], **EXACT)
        delta[...] = first
        gifts.copies[0].start()
        part[...] = cross_product(first, side[...])
        gifts.copies[1].start()
        share(first)
        gifts.drain()

    @pl.when(c == 1)
    def _():
        arrive(gifts.copies[:1])
        here = cross_product(other[...], side[...])
        arrive(gifts.copies[1:])
        cross = jnp.concatenate([opart[...], here], axis=1)
        share(jnp.dot(prod[...].reshape(64, BLOCK) - cross, inv[...], **EXACT))

    out.drain()


def update(block_ids, landmarks, features, labels, scores, ridge):
    rows = features.shape[0]
    share = landmarks.shape[0] // 8
    vmem = pl.BlockSpec(memory_space=pltpu.VMEM)
    wide = lambda *shape: pltpu.VMEM(shape, F32)
    half = lambda *shape: pltpu.VMEM(shape, BF16)
    return pl.pallas_call(
        functools.partial(update_kernel, ridge),
        out_shape=(
            jax.ShapeDtypeStruct((rows, 2 * BLOCK), BF16),
            jax.ShapeDtypeStruct((2, NX, NY, 64, BLOCK), BF16),
        ),
        in_specs=[pl.BlockSpec(memory_space=pltpu.SMEM)] + [pl.BlockSpec(memory_space=pltpu.HBM)] * 4,
        out_specs=(vmem,) * 2,
        scratch_shapes=[
            half(share, 1024),
            half(rows, 1024),
            pltpu.VMEM((1, rows), jnp.int32),
            half(rows, scores.shape[1]),
            pltpu.SemaphoreType.DMA((4,)),
            half(NY, NZ, 16, 256),
            half(rows, 1024),
            half(rows, CLASSES),
            half(NY, 2, NX, 2, 4, 16, 256),
            half(rows, 1024),
            half(rows, CLASSES),
            half(NY - 1, NZ, 16, 256),
            half(NZ, 16, 256),
            half(NZ - 1, 16, 256),
            half(2 * rows, 2 * BLOCK),
            wide(NX, NY, NZ, 16, TILE),
            wide(8, TILE),
            wide(NX, NY, 64, BLOCK),
            wide(3, 4, 4, 16, TILE),
            wide(3, 4, 4, 16, TILE),
            wide(4, 4, 16, TILE),
            wide(4, 4, 16, TILE),
            wide(3, 4, 16, TILE),
            wide(3, 4, 16, TILE),
            wide(NZ, 16, TILE),
            wide(NZ - 1, 16, TILE),
            wide(NX, NY, NZ, 16, TILE),
            wide(3, 8, TILE),
            wide(8, TILE),
            wide(3, 8, TILE),
            wide(8, TILE),
            wide(NZ - 1, 8, TILE),
            wide(3, 4, 32, BLOCK),
            wide(3, 4, 32, BLOCK),
            wide(4, 32, BLOCK),
            wide(4, 32, BLOCK),
            wide(3, 32, BLOCK),
            wide(3, 32, BLOCK),
            wide(NZ, 8, BLOCK),
            wide(NZ - 1, 8, BLOCK),
            wide(NZ, 8, BLOCK),
            wide(BLOCK, BLOCK),
            wide(TILE, BLOCK),
            wide(256, BLOCK),
            wide(64, BLOCK),
            wide(64, 256),
            wide(64, BLOCK),
            wide(64, 256),
            pltpu.SemaphoreType.DMA((COPIES,)),
            pltpu.SemaphoreType.DMA((COPIES,)),
        ],
        compiler_params=pltpu.CompilerParams(
            collective_id=0, has_side_effects=True, vmem_limit_bytes=VMEM_LIMIT
        ),
        name="update",
    )(block_ids, landmarks, features, labels, scores)


def finish_kernel(block_ids, kern, deltas, labels, scores, old, new, residual, old_tiles, new_tiles, rest, fetch_sems, store_sems):
    count = scores.shape[1]
    holder = lax.axis_index("rows")
    size = count // 5
    parts = [slice(i * size, (i + 1) * size) for i in range(5)]
    fetches = [
        pltpu.make_async_copy(old.at[parts[i]], old_tiles.at[i], fetch_sems.at[i]) for i in range(5)
    ]
    for fetch in fetches:
        fetch.start()
    total = onehot(labels[...], scores.shape) - scores[...].astype(F32)
    last = (((1,), (1,)), ((), ()))
    for s in range(2):
        moved = lax.dot_general(
            kern[:, s * BLOCK : (s + 1) * BLOCK], deltas[s], last, preferred_element_type=F32
        )
        total = total - moved[:, :count]
    rest[...] = total
    stores = [pltpu.make_async_copy(rest, residual, store_sems.at[5])]
    stores[0].start()
    held = [jnp.where(block_ids[s] == holder, 1.0, 0.0) for s in range(2)]
    for i in range(5):
        added = [deltas[s, parts[i], :].astype(F32) * held[s] for s in range(2)]
        fetches[i].wait()
        new_tiles[i] = old_tiles[i] + (added[0] + added[1])
        stores.append(pltpu.make_async_copy(new_tiles.at[i], new.at[parts[i]], store_sems.at[i]))
        stores[-1].start()
    for store in stores:
        store.wait()


def finish(block_ids, kern, deltas, labels, scores, coefficients):
    vmem = pl.BlockSpec(memory_space=pltpu.VMEM)
    hbm = pl.BlockSpec(memory_space=pltpu.HBM)
    count = scores.shape[1]
    return pl.pallas_call(
        finish_kernel,
        out_shape=(
            jax.ShapeDtypeStruct(coefficients.shape, F32),
            jax.ShapeDtypeStruct(scores.shape, F32),
        ),
        in_specs=[pl.BlockSpec(memory_space=pltpu.SMEM)] + [vmem] * 4 + [hbm],
        out_specs=(hbm,) * 2,
        scratch_shapes=[
            pltpu.VMEM((5, count // 5, BLOCK), F32),
            pltpu.VMEM((5, count // 5, BLOCK), F32),
            pltpu.VMEM(scores.shape, F32),
            pltpu.SemaphoreType.DMA((5,)),
            pltpu.SemaphoreType.DMA((6,)),
        ],
        compiler_params=pltpu.CompilerParams(vmem_limit_bytes=VMEM_LIMIT),
        name="finish",
    )(block_ids, kern, deltas, labels, scores, coefficients)


def shards(features, labels, scores, landmarks, coefficients, block_ids):
    devices_all = lax.axis_size("rows") * lax.axis_size("rrep")
    ridge = float(features.shape[0] * devices_all)
    labels = labels[None, :]
    kern, deltas = update(block_ids, landmarks, features, labels, scores, ridge)
    deltas = deltas.reshape(2, CLASSES, BLOCK)
    new, residual = finish(block_ids, kern, deltas, labels, scores, coefficients.T)
    return new.T, residual


def solution(mesh):
    in_specs = (
        P(("rows", "rrep"), None),
        P(("rows", "rrep")),
        P(("rows", "rrep"), None),
        P("rows", None),
        P("rows", None),
        P(),
    )
    out_specs = (P("rows", None), P(("rows", "rrep"), None))
    return jax.shard_map(shards, mesh=mesh, in_specs=in_specs, out_specs=out_specs, check_vma=False)
```
